256 devices in a mesh: inner: 8 (over x, y_hi), outer: 32 (over y_lo, z, core).
Axes of the slice: x: 4, y: 4 (y_hi: 2, y_lo: 2; y = y_hi * 2 + y_lo), z: 8, core: 2. Of those that a mesh axis runs over, the one named last changes fastest.
Arguments:
- queries: bfloat16 [32768, 8192], P(('inner', 'outer')), may hold values from -6 to 6
- keys: bfloat16 [32768, 1024], P(('inner', 'outer')), may hold values from -6 to 6
- values: bfloat16 [32768, 1024], P(('inner', 'outer')), may hold values from -6 to 6
- documents: int32 [32768], P(('inner', 'outer')), may hold values from 0 to 127, never falling along the last dimension, each value on 1 to 512 neighbouring positions
Outputs:
- attended: bfloat16 [32768, 8192], P(('inner', 'outer'))
The draws below stay inside these ranges and needn't reach their ends.
Inputs may be any that keep to these rules, and one draw needn't show every extreme that they name: `documents`: non-decreasing along the sequence; every document spans 1 to 512 tokens, one exactly 512.
All inputs are finite; a program needn't handle non-finite values.
Results may differ from the reference program's by a relative error of at most 0.0045.
Values may be sent and summed in bfloat16 or wider, within the bound.
A program may use at most 64 MiB of HBM per device.

```python
import math
import jax
import jax.numpy as jnp
import numpy as np
from jax import lax

QUERY_HEADS = 64
KEY_VALUE_HEADS = 8
HEAD_SIZE = 128
DEVICE_TOKENS = 128
PACKED_TOKENS = 32768
MOST = 512
REACH = 4
DOCS = 128


def draw_queries(key, part):
    key = jax.random.fold_in(key, 11)
    second_factor = jax.random.fold_in(key, 1)
    base_offset = jnp.clip(jax.random.normal(second_factor, (PACKED_TOKENS, QUERY_HEADS * HEAD_SIZE), jnp.float32), -6.0, 6.0)
    return base_offset.astype(jnp.bfloat16)


def draw_keys(key, part):
    key = jax.random.fold_in(key, 12)
    second_factor = jax.random.fold_in(key, 1)
    base_offset = jnp.clip(jax.random.normal(second_factor, (PACKED_TOKENS, KEY_VALUE_HEADS * HEAD_SIZE), jnp.float32), -6.0, 6.0)
    return base_offset.astype(jnp.bfloat16)


def levels(rng, shape, shards, least, high):
    level, own = 1.0, jax.random.fold_in(rng, 6)
    for dim, blocks in shards:
        draws = jnp.exp(jax.random.uniform(jax.random.fold_in(own, dim), (blocks,), jnp.float32, least / len(shards), high / len(shards)))
        level = level * jnp.repeat(draws, shape[dim] // blocks).reshape([-1 if axis == dim else 1 for axis in range(len(shape))])
    return level


def split_up(number_of, total, most, skew):
    loads = [(1 << 20) // math.isqrt(standing ** skew) + 1 for standing in range(2, number_of + 1)]
    spare, holding = total - most - (number_of - 1), [1] * (number_of - 1)
    while spare > 0:
        free = [i for i in range(number_of - 1) if holding[i] < most]
        mass, left = sum([loads[i] for i in free]), spare
        for i in free:
            addition = min(most - holding[i], max(1, left * loads[i] // mass), spare)
            holding[i] = holding[i] + addition
            spare = spare - addition
    return np.array([most] + holding)


def uneven_parts(stream_key, number_of, total, most, skew):
    if number_of == 2:
        one = jax.random.randint(stream_key, (), max(1, total - most), min(most, total - 1) + 1)
        return jnp.stack([one, total - one])
    sizes = jnp.asarray(split_up(number_of, total, most, skew), jnp.int32)
    couples = (number_of - 1) // 2
    donor, receiver = sizes[1:1 + 2 * couples:2], sizes[2:2 + 2 * couples:2]
    margin = jnp.minimum(donor - 1, most - receiver)
    shifted = jax.random.randint(jax.random.fold_in(stream_key, 1), (couples,), 0, 1 << 20) % (margin + 1)
    sizes = sizes.at[1:1 + 2 * couples:2].set(donor - shifted).at[2:2 + 2 * couples:2].set(receiver + shifted)
    return sizes[jax.random.permutation(jax.random.fold_in(stream_key, 2), number_of)]


def scatter_about(own_key, shape, deviation, most, cuts=(), kind=jnp.bfloat16):
    values = deviation * jax.random.normal(own_key, shape, jnp.float32)
    if cuts:
        values = values * levels(own_key, shape, cuts, -0.22, 0.18)
    return jnp.clip(values, -most, most).astype(kind)


def setup_inputs(seed: int = 0) -> dict:
    arg_keys = jax.random.split(jax.random.key(seed), 5)
    return {
        "queries": draw_queries(jax.random.fold_in(arg_keys[4], 71), 0),
        "keys": draw_keys(jax.random.fold_in(arg_keys[4], 71), 0),
        "values": scatter_about(arg_keys[2], (PACKED_TOKENS, KEY_VALUE_HEADS * HEAD_SIZE), 1.0, 6.0, ((0, 256),)),
        "documents": jnp.searchsorted(jnp.cumsum(uneven_parts(arg_keys[3], DOCS, PACKED_TOKENS, MOST, 2)), jnp.arange(PACKED_TOKENS), side="right").astype(jnp.int32),
    }


def reference(queries, keys, values, documents):
    padding_width = REACH * DEVICE_TOKENS
    window_length = padding_width + DEVICE_TOKENS
    group_ratio = QUERY_HEADS // KEY_VALUE_HEADS
    padded_keys = jnp.concatenate([jnp.zeros((padding_width, KEY_VALUE_HEADS * HEAD_SIZE), jnp.bfloat16), keys], axis=0)
    padded_values = jnp.concatenate([jnp.zeros((padding_width, KEY_VALUE_HEADS * HEAD_SIZE), jnp.bfloat16), values], axis=0)
    doc_pad = jnp.concatenate([-jnp.ones((padding_width,), jnp.int32), documents], axis=0)
    scale = HEAD_SIZE ** -0.5

    def one_block(block):
        start_index = (block * DEVICE_TOKENS).astype(jnp.int32)
        query_rows = lax.dynamic_slice_in_dim(queries, start_index, DEVICE_TOKENS, 0).reshape(DEVICE_TOKENS, KEY_VALUE_HEADS, group_ratio, HEAD_SIZE)
        key_window_rows = lax.dynamic_slice_in_dim(padded_keys, start_index, window_length, 0).reshape(window_length, KEY_VALUE_HEADS, HEAD_SIZE)
        value_window_rows = lax.dynamic_slice_in_dim(padded_values, start_index, window_length, 0).reshape(window_length, KEY_VALUE_HEADS, HEAD_SIZE)
        doc_query = lax.dynamic_slice_in_dim(documents, start_index, DEVICE_TOKENS, 0)
        doc_key = lax.dynamic_slice_in_dim(doc_pad, start_index, window_length, 0)
        score = jnp.einsum("qgrd,kgd->grqk", query_rows.astype(jnp.float32), key_window_rows.astype(jnp.float32)) * scale
        query_pos = jnp.arange(DEVICE_TOKENS, dtype=jnp.int32) + padding_width
        key_pos = jnp.arange(window_length, dtype=jnp.int32)
        allowed = (doc_query[:, None] == doc_key[None, :]) & (key_pos[None, :] <= query_pos[:, None])
        score = jnp.where(allowed, score, -1e30)
        top = jnp.max(score, axis=-1, keepdims=True)
        weight = jnp.where(allowed, jnp.exp(score - top), 0.0)
        total = jnp.sum(weight, axis=-1)
        weight_b = weight.astype(jnp.bfloat16)
        mixed = jnp.einsum("grqk,kgd->qgrd", weight_b.astype(jnp.float32), value_window_rows.astype(jnp.float32))
        mixed = mixed / jnp.transpose(total, (2, 0, 1))[..., None]
        return mixed.reshape(DEVICE_TOKENS, QUERY_HEADS * HEAD_SIZE).astype(jnp.bfloat16)

    blocks = lax.map(one_block, jnp.arange(PACKED_TOKENS // DEVICE_TOKENS, dtype=jnp.int32))
    return blocks.reshape(PACKED_TOKENS, QUERY_HEADS * HEAD_SIZE)
```

```python
import functools

import jax
import jax.numpy as jnp
from jax import lax
from jax.experimental import pallas as pl
from jax.experimental.pallas import tpu as pltpu
from jax.sharding import PartitionSpec as P

MESH = pl.DeviceIdType.MESH
HEAD = 128
GROUPS = 8
RATIO = 8
TOK = 128
OWN = 4
AHEAD = 3
MASKED = -1e30
LINK, RELAY, PAIR_NEAR, PAIR_FAR = range(4)
LOG2E = 1.4426950408889634


def kernel(n, outer, q_hbm, k_hbm, v_hbm, doc_ref, o_hbm, kv, tag, qv, ov, bias, in_sem, q_sem, o_sem, send, recv, tsend, trecv):
    b = lax.axis_index("inner") * outer + lax.axis_index("outer")
    core = lax.rem(b, 2)
    sibling = b + 1 - 2 * core
    after = lax.rem(b + 2, n)
    before = lax.rem(b + n - 2, n)

    def at(device):
        return (device // outer, lax.rem(device, outer))

    def load(g):
        cols = pl.ds(pl.multiple_of(g * HEAD, HEAD), HEAD)
        return (
            pltpu.make_async_copy(k_hbm.at[:, cols], kv.at[g, OWN, pl.ds(0, TOK)], in_sem.at[g, 0]),
            pltpu.make_async_copy(v_hbm.at[:, cols], kv.at[g, OWN, pl.ds(TOK, TOK)], in_sem.at[g, 1]),
        )

    def load_q(g):
        cols = pl.ds(pl.multiple_of(g * RATIO * HEAD, HEAD), RATIO * HEAD)
        return pltpu.make_async_copy(q_hbm.at[:, cols], qv.at[g], q_sem.at[g])

    def store(g):
        cols = pl.ds(pl.multiple_of(g * RATIO * HEAD, HEAD), RATIO * HEAD)
        return pltpu.make_async_copy(ov.at[g], o_hbm.at[:, cols], o_sem.at[g])

    near_src = OWN - 2 * core
    far_src = 2 - 2 * core
    routes = {
        LINK: (OWN, 2, after),
        RELAY: (2, 0, after),
        PAIR_NEAR: (near_src, 3, sibling),
        PAIR_FAR: (far_src, 1, sibling),
    }

    def move(kind, g):
        src, dst, device = routes[kind]
        return pltpu.make_async_remote_copy(
            src_ref=kv.at[g, src],
            dst_ref=kv.at[g, dst],
            send_sem=send.at[kind, g],
            recv_sem=recv.at[kind, g],
            device_id=at(device),
            device_id_type=MESH,
        )

    def move_tag(kind):
        src, dst, device = routes[kind]
        return pltpu.make_async_remote_copy(
            src_ref=tag.at[src],
            dst_ref=tag.at[dst],
            send_sem=tsend.at[kind],
            recv_sem=trecv.at[kind],
            device_id=at(device),
            device_id_type=MESH,
        )

    for g in range(GROUPS):
        for c in load(g):
            c.start()
    for g in range(GROUPS):
        load_q(g).start()

    barrier = pltpu.get_barrier_semaphore()
    pl.semaphore_signal(barrier, inc=1, device_id=at(before), device_id_type=MESH)
    pl.semaphore_signal(barrier, inc=1, device_id=at(sibling), device_id_type=MESH)

    docs = jnp.broadcast_to(doc_ref[...].reshape(1, TOK).astype(jnp.float32), (TOK, TOK))
    tag[OWN] = docs[:16].astype(jnp.bfloat16)
    column = docs.T

    pl.semaphore_wait(barrier, 2)
    move_tag(LINK).start()
    for g in range(AHEAD):
        for c in load(g):
            c.wait()
        move(LINK, g).start()
    move_tag(LINK).wait_recv()
    move_tag(RELAY).start()
    move_tag(PAIR_NEAR).start()
    move_tag(RELAY).wait_recv()
    move_tag(PAIR_FAR).start()
    row = lax.broadcasted_iota(jnp.int32, (TOK, TOK), 0)
    col = lax.broadcasted_iota(jnp.int32, (TOK, TOK), 1)
    bias[:, OWN * TOK :] = jnp.where((column == docs) & (col <= row), 0.0, MASKED)
    move_tag(PAIR_NEAR).wait_recv()
    move_tag(PAIR_FAR).wait_recv()
    for s in range(OWN):
        other = jnp.broadcast_to(tag[s][:1].astype(jnp.float32), (TOK, TOK))
        bias[:, s * TOK : (s + 1) * TOK] = jnp.where(column == other, 0.0, MASKED)

    ones = jnp.ones((5 * TOK, HEAD), jnp.bfloat16)

    def compute(g):
        load_q(g).wait()
        k = kv[g, :, :TOK, :].reshape(5 * TOK, HEAD)
        va = jnp.concatenate([kv[g, :, TOK:, :].reshape(5 * TOK, HEAD), ones], axis=1)
        for h in range(RATIO):
            q = qv[g, :, h * HEAD : (h + 1) * HEAD]
            s = lax.dot_general(q, k, (((1,), (1,)), ((), ())), preferred_element_type=jnp.float32)
            t = s * (HEAD**-0.5 * LOG2E) + bias[...]
            p = jnp.exp2(t - jnp.max(t, axis=-1, keepdims=True)).astype(jnp.bfloat16)
            acc = jnp.dot(p, va, preferred_element_type=jnp.float32)
            ov[g, :, h * HEAD : (h + 1) * HEAD] = (acc[:, :HEAD] / acc[:, HEAD:]).astype(jnp.bfloat16)
        store(g).start()

    def step(it, _):
        @pl.when(it < GROUPS)
        def _():
            move(LINK, it).wait_recv()
            move(RELAY, it).start()
            move(PAIR_NEAR, it).start()

        @pl.when(it + AHEAD < GROUPS)
        def _():
            for c in load(it + AHEAD):
                c.wait()
            move(LINK, it + AHEAD).start()

        @pl.when((it >= 1) & (it < GROUPS + 1))
        def _():
            move(RELAY, it - 1).wait_recv()
            move(PAIR_FAR, it - 1).start()

        @pl.when(it >= 2)
        def _():
            move(PAIR_NEAR, it - 2).wait_recv()
            move(PAIR_FAR, it - 2).wait_recv()
            compute(it - 2)

        return 0

    lax.fori_loop(0, GROUPS + 2, step, 0)

    for kind in routes:
        move_tag(kind).wait_send()

    def finish(g, _):
        for kind in routes:
            move(kind, g).wait_send()
        store(g).wait()
        return 0

    lax.fori_loop(0, GROUPS, finish, 0)


def solution(mesh):
    n, outer = mesh.size, mesh.shape["outer"]

    def local(queries, keys, values, documents):
        anywhere = pl.BlockSpec(memory_space=pl.ANY)
        return pl.pallas_call(
            functools.partial(kernel, n, outer),
            out_shape=jax.ShapeDtypeStruct(queries.shape, jnp.bfloat16),
            in_specs=[anywhere, anywhere, anywhere, pl.BlockSpec(memory_space=pltpu.VMEM)],
            out_specs=anywhere,
            scratch_shapes=[
                pltpu.VMEM((GROUPS, 5, 2 * TOK, HEAD), jnp.bfloat16),
                pltpu.VMEM((5, 16, TOK), jnp.bfloat16),
                pltpu.VMEM((GROUPS, TOK, RATIO * HEAD), jnp.bfloat16),
                pltpu.VMEM((GROUPS, TOK, RATIO * HEAD), jnp.bfloat16),
                pltpu.VMEM((TOK, 5 * TOK), jnp.float32),
                pltpu.SemaphoreType.DMA((GROUPS, 2)),
                pltpu.SemaphoreType.DMA((GROUPS,)),
                pltpu.SemaphoreType.DMA((GROUPS,)),
                pltpu.SemaphoreType.DMA((4, GROUPS)),
                pltpu.SemaphoreType.DMA((4, GROUPS)),
                pltpu.SemaphoreType.DMA((4,)),
                pltpu.SemaphoreType.DMA((4,)),
            ],
            name="packed_attention",
            compiler_params=pltpu.CompilerParams(
                collective_id=0, has_side_effects=True, vmem_limit_bytes=60 * 2**20
            ),
            cost_estimate=pl.CostEstimate(flops=2_684_354_560, bytes_accessed=4_718_592, transcendentals=5_242_880),
        )(queries, keys, values, documents)

    row = P(("inner", "outer"), None)
    return jax.shard_map(local, mesh=mesh, in_specs=(row, row, row, P(("inner", "outer"))), out_specs=row, check_vma=False)
```

```python
import functools

import jax
import jax.numpy as jnp
from jax import lax
from jax.experimental import pallas as pl
from jax.experimental.pallas import tpu as pltpu
from jax.sharding import PartitionSpec as P

MESH = pl.DeviceIdType.MESH
HEAD = 128
GROUPS = 8
RATIO = 8
TOK = 128
OWN = 4
AHEAD = 4
LAG = 3
FIRST = GROUPS - 1
MASKED = -1e30
LINK, RELAY, PAIR_NEAR, PAIR_FAR = range(4)
LOG2E = 1.4426950408889634


def group_columns(g):
    return pl.ds(pl.multiple_of(g * RATIO * HEAD, HEAD), RATIO * HEAD)


def attend(q_at, kv_at, bias, out_at):
    k = kv_at[:, :TOK, :].reshape(5 * TOK, HEAD)
    v = kv_at[:, TOK:, :].reshape(5 * TOK, HEAD)
    v = jnp.concatenate([v, jnp.ones_like(v)], axis=1)
    for h in range(RATIO):
        cols = slice(h * HEAD, (h + 1) * HEAD)
        s = lax.dot_general(q_at[:, cols], k, (((1,), (1,)), ((), ())), preferred_element_type=jnp.float32)
        t = s * (HEAD**-0.5 * LOG2E) + bias[...]
        p = jnp.exp2(t - jnp.max(t, axis=-1, keepdims=True)).astype(jnp.bfloat16)
        acc = jnp.dot(p, v, preferred_element_type=jnp.float32)
        out_at[:, cols] = (acc[:, :HEAD] / acc[:, HEAD:]).astype(jnp.bfloat16)


def first_kernel(n, outer, q_hbm, k_hbm, v_hbm, doc_hbm, part, kv, qv, bias, doc, tag, in_sem, q_sem, d_sem, send, recv, tsend, trecv):
    b = lax.axis_index("inner") * outer + lax.axis_index("outer")
    core = lax.rem(b, 2)
    sibling = b + 1 - 2 * core
    has_next = b < n - 2
    has_prev = b >= 2
    has_two = b >= 4
    after = jnp.minimum(b + 2, n - 2 + core)
    before = jnp.maximum(b - 2, core)

    def at(device):
        return (device // outer, lax.rem(device, outer))

    def load(g):
        cols = pl.ds(pl.multiple_of(g * HEAD, HEAD), HEAD)
        return (
            pltpu.make_async_copy(k_hbm.at[:, cols], kv.at[g, OWN, pl.ds(0, TOK)], in_sem.at[g, 0]),
            pltpu.make_async_copy(v_hbm.at[:, cols], kv.at[g, OWN, pl.ds(TOK, TOK)], in_sem.at[g, 1]),
        )

    def load_q(g):
        return pltpu.make_async_copy(q_hbm.at[:, group_columns(g)], qv.at[g], q_sem.at[g])

    near_src = OWN - 2 * core
    far_src = 2 - 2 * core
    routes = {
        LINK: (OWN, 2, after),
        RELAY: (2, 0, after),
        PAIR_NEAR: (near_src, 3, sibling),
        PAIR_FAR: (far_src, 1, sibling),
    }

    def move(kind, g):
        src, dst, device = routes[kind]
        return pltpu.make_async_remote_copy(
            src_ref=kv.at[g, src],
            dst_ref=kv.at[g, dst],
            send_sem=send.at[kind, g],
            recv_sem=recv.at[kind, g],
            device_id=at(device),
            device_id_type=MESH,
        )

    def move_tag(kind):
        src, dst, device = routes[kind]
        return pltpu.make_async_remote_copy(
            src_ref=tag.at[src],
            dst_ref=tag.at[dst],
            send_sem=tsend.at[kind],
            recv_sem=trecv.at[kind],
            device_id=at(device),
            device_id_type=MESH,
        )

    doc_copy = pltpu.make_async_copy(doc_hbm, doc, d_sem)
    doc_copy.start()
    for g in range(GROUPS):
        for c in load(g):
            c.start()
    for g in range(GROUPS):
        load_q(g).start()

    barrier = pltpu.get_barrier_semaphore()

    @pl.when(has_prev)
    def _():
        pl.semaphore_signal(barrier, inc=1, device_id=at(before), device_id_type=MESH)

    pl.semaphore_signal(barrier, inc=1, device_id=at(sibling), device_id_type=MESH)

    @pl.when(jnp.logical_not(has_two))
    def _():
        kv[:, 0] = jnp.zeros((GROUPS, 2 * TOK, HEAD), jnp.bfloat16)
        tag[0] = jnp.full((16, TOK), -1, jnp.bfloat16)

    @pl.when(jnp.logical_not(has_prev))
    def _():
        kv[:, 2] = jnp.zeros((GROUPS, 2 * TOK, HEAD), jnp.bfloat16)
        tag[2] = jnp.full((16, TOK), -1, jnp.bfloat16)

    doc_copy.wait()
    docs = jnp.broadcast_to(doc[...].reshape(1, TOK).astype(jnp.float32), (TOK, TOK))
    tag[OWN] = docs[:16].astype(jnp.bfloat16)
    column = docs.T

    def when(condition, action):
        pl.when(condition)(action)

    pl.semaphore_wait(barrier, 1 + has_next.astype(jnp.int32))
    when(has_next, lambda: move_tag(LINK).start())
    for g in range(AHEAD):
        for c in load(g):
            c.wait()
        when(has_next, lambda: move(LINK, g).start())
    when(has_prev, lambda: move_tag(LINK).wait_recv())
    when(has_prev & has_next, lambda: move_tag(RELAY).start())
    move_tag(PAIR_NEAR).start()
    row = lax.broadcasted_iota(jnp.int32, (TOK, TOK), 0)
    col = lax.broadcasted_iota(jnp.int32, (TOK, TOK), 1)
    bias[:, OWN * TOK :] = jnp.where((column == docs) & (col <= row), 0.0, MASKED)
    when(has_two, lambda: move_tag(RELAY).wait_recv())
    move_tag(PAIR_FAR).start()
    move_tag(PAIR_NEAR).wait_recv()
    move_tag(PAIR_FAR).wait_recv()
    for s in range(OWN):
        other = jnp.broadcast_to(tag[s][:1].astype(jnp.float32), (TOK, TOK))
        bias[:, s * TOK : (s + 1) * TOK] = jnp.where(column == other, 0.0, MASKED)

    def step(it, _):
        @pl.when(it < GROUPS)
        def _():
            when(has_prev, lambda: move(LINK, it).wait_recv())
            when(has_prev & has_next, lambda: move(RELAY, it).start())
            move(PAIR_NEAR, it).start()

        @pl.when(it + AHEAD < GROUPS)
        def _():
            for c in load(it + AHEAD):
                c.wait()
            when(has_next, lambda: move(LINK, it + AHEAD).start())

        @pl.when((it >= LAG) & (it < GROUPS + LAG))
        def _():
            when(has_two, lambda: move(RELAY, it - LAG).wait_recv())
            move(PAIR_FAR, it - LAG).start()

        @pl.when(it > LAG)
        def _():
            g = it - LAG - 1
            move(PAIR_NEAR, g).wait_recv()
            move(PAIR_FAR, g).wait_recv()
            load_q(g).wait()
            attend(qv.at[g], kv.at[g], bias, part.at[g])

        return 0

    lax.fori_loop(0, FIRST + LAG + 1, step, 0)

    for kind in routes:
        if kind == LINK:
            when(has_next, lambda: move_tag(LINK).wait_send())
        elif kind == RELAY:
            when(has_prev & has_next, lambda: move_tag(RELAY).wait_send())
        else:
            move_tag(kind).wait_send()

    def finish(g, _):
        when(has_next, lambda: move(LINK, g).wait_send())
        when(has_prev & has_next, lambda: move(RELAY, g).wait_send())
        move(PAIR_NEAR, g).wait_send()
        move(PAIR_FAR, g).wait_send()
        return 0

    lax.fori_loop(0, GROUPS, finish, 0)
    for g in range(FIRST, GROUPS):
        load_q(g).wait()
        move(PAIR_NEAR, g).wait_recv()
        move(PAIR_FAR, g).wait_recv()


def last_kernel(part, kv, qv, bias, o_hbm, out, sem):
    def store(g):
        source = part.at[g] if g < FIRST else out.at[g - FIRST]
        return pltpu.make_async_copy(source, o_hbm.at[:, group_columns(g)], sem.at[g])

    for g in range(FIRST):
        store(g).start()
    for g in range(FIRST, GROUPS):
        attend(qv.at[g], kv.at[g], bias, out.at[g - FIRST])
        store(g).start()
    for g in range(GROUPS):
        store(g).wait()


def solution(mesh):
    n, outer = mesh.size, mesh.shape["outer"]

    def local(queries, keys, values, documents):
        anywhere = pl.BlockSpec(memory_space=pl.ANY)
        vmem = pl.BlockSpec(memory_space=pltpu.VMEM)
        arguments = [pltpu.with_memory_space_constraint(x, pltpu.HBM) for x in (queries, keys, values, documents)]
        part, kv, qv, bias = pl.pallas_call(
            functools.partial(first_kernel, n, outer),
            out_shape=(
                pltpu.VMEM((FIRST, TOK, RATIO * HEAD), jnp.bfloat16),
                pltpu.VMEM((GROUPS, 5, 2 * TOK, HEAD), jnp.bfloat16),
                pltpu.VMEM((GROUPS, TOK, RATIO * HEAD), jnp.bfloat16),
                pltpu.VMEM((TOK, 5 * TOK), jnp.float32),
            ),
            in_specs=[anywhere] * 4,
            out_specs=(vmem,) * 4,
            scratch_shapes=[
                pltpu.VMEM((TOK,), jnp.int32),
                pltpu.VMEM((5, 16, TOK), jnp.bfloat16),
                pltpu.SemaphoreType.DMA((GROUPS, 2)),
                pltpu.SemaphoreType.DMA((GROUPS,)),
                pltpu.SemaphoreType.DMA,
                pltpu.SemaphoreType.DMA((4, GROUPS)),
                pltpu.SemaphoreType.DMA((4, GROUPS)),
                pltpu.SemaphoreType.DMA((4,)),
                pltpu.SemaphoreType.DMA((4,)),
            ],
            name="relay_and_attend",
            compiler_params=pltpu.CompilerParams(
                collective_id=0, has_side_effects=True, vmem_limit_bytes=24 * 2**20
            ),
        )(*arguments)
        return pl.pallas_call(
            last_kernel,
            out_shape=jax.ShapeDtypeStruct(queries.shape, jnp.bfloat16),
            in_specs=[vmem] * 4,
            out_specs=anywhere,
            scratch_shapes=[
                pltpu.VMEM((GROUPS - FIRST, TOK, RATIO * HEAD), jnp.bfloat16),
                pltpu.SemaphoreType.DMA((GROUPS,)),
            ],
            name="attend_and_write",
            compiler_params=pltpu.CompilerParams(vmem_limit_bytes=24 * 2**20),
        )(part, kv, qv, bias)

    row = P(("inner", "outer"), None)
    return jax.shard_map(local, mesh=mesh, in_specs=(row, row, row, P(("inner", "outer"))), out_specs=row, check_vma=False)
```

```python
import functools

import jax
import jax.numpy as jnp
from jax import lax
from jax.experimental import pallas as pl
from jax.experimental.pallas import tpu as pltpu
from jax.sharding import PartitionSpec as P

MESH = pl.DeviceIdType.MESH
HEAD = 128
GROUPS = 8
RATIO = 8
TOK = 128
OWN = 4
AHEAD = 4
LAG = 3
DIVERT = 6
KEPT = GROUPS - DIVERT
FIRST = GROUPS - 1
MASKED = -1e30
LINK, RELAY, PAIR_NEAR, PAIR_FAR = range(4)
LOG2E = 1.4426950408889634


def group_columns(g):
    return pl.ds(pl.multiple_of(g * RATIO * HEAD, HEAD), RATIO * HEAD)


def attend(q_at, kv_at, bias, out_at):
    k = kv_at[:, :TOK, :].reshape(5 * TOK, HEAD)
    v = kv_at[:, TOK:, :].reshape(5 * TOK, HEAD)
    v = jnp.concatenate([v, jnp.ones_like(v)], axis=1)
    for h in range(RATIO):
        cols = slice(h * HEAD, (h + 1) * HEAD)
        s = lax.dot_general(q_at[:, cols], k, (((1,), (1,)), ((), ())), preferred_element_type=jnp.float32)
        t = s * (HEAD**-0.5 * LOG2E) + bias[...]
        p = jnp.exp2(t - jnp.max(t, axis=-1, keepdims=True)).astype(jnp.bfloat16)
        acc = jnp.dot(p, v, preferred_element_type=jnp.float32)
        out_at[:, cols] = (acc[:, :HEAD] / acc[:, HEAD:]).astype(jnp.bfloat16)


def first_kernel(n, outer, q_hbm, k_hbm, v_hbm, doc_hbm, part, kv, qv, bias, doc, column, tag, mid, in_sem, q_sem, d_sem, send, recv, tsend, trecv, dsend, drecv):
    b = lax.axis_index("inner") * outer + lax.axis_index("outer")
    core = lax.rem(b, 2)
    sibling = b + 1 - 2 * core
    has_next = b < n - 2
    has_prev = b >= 2
    has_two = b >= 4
    z = lax.rem(b // 2, 8)
    more_rows = b < n - 16
    is_source = (z == 6) & more_rows
    is_middle = (z == 3) & (b >= 16)
    is_target = (z == 0) & (b >= 16)
    after = jnp.minimum(b + 2, n - 2 + core)
    before = jnp.maximum(b - 2, core)

    def at(device):
        return (device // outer, lax.rem(device, outer))

    def load(g):
        cols = pl.ds(pl.multiple_of(g * HEAD, HEAD), HEAD)
        return (
            pltpu.make_async_copy(k_hbm.at[:, cols], kv.at[g, OWN, pl.ds(0, TOK)], in_sem.at[g, 0]),
            pltpu.make_async_copy(v_hbm.at[:, cols], kv.at[g, OWN, pl.ds(TOK, TOK)], in_sem.at[g, 1]),
        )

    def load_q(g):
        return pltpu.make_async_copy(q_hbm.at[:, group_columns(g)], qv.at[g], q_sem.at[g])

    near_src = OWN - 2 * core
    far_src = 2 - 2 * core
    routes = {
        LINK: (OWN, 2, after),
        RELAY: (2, 0, after),
        PAIR_NEAR: (near_src, 3, sibling),
        PAIR_FAR: (far_src, 1, sibling),
    }

    def move(kind, g):
        src, dst, device = routes[kind]
        return pltpu.make_async_remote_copy(
            src_ref=kv.at[g, src],
            dst_ref=kv.at[g, dst],
            send_sem=send.at[kind, g],
            recv_sem=recv.at[kind, g],
            device_id=at(device),
            device_id_type=MESH,
        )

    def move_tag(kind):
        src, dst, device = routes[kind]
        return pltpu.make_async_remote_copy(
            src_ref=tag.at[src],
            dst_ref=tag.at[dst],
            send_sem=tsend.at[kind],
            recv_sem=trecv.at[kind],
            device_id=at(device),
            device_id_type=MESH,
        )

    def to_middle(m):
        return pltpu.make_async_remote_copy(
            src_ref=kv.at[KEPT + m, OWN],
            dst_ref=mid.at[m],
            send_sem=dsend.at[0, m],
            recv_sem=drecv.at[m],
            device_id=at(jnp.minimum(b + 10, n - 1)),
            device_id_type=MESH,
        )

    def from_middle(m):
        return pltpu.make_async_remote_copy(
            src_ref=mid.at[m],
            dst_ref=kv.at[KEPT + m, 0],
            send_sem=dsend.at[1, m],
            recv_sem=recv.at[RELAY, KEPT + m],
            device_id=at(jnp.maximum(b - 6, 0)),
            device_id_type=MESH,
        )

    def relays(g):
        return has_prev & has_next & jnp.logical_not((z == 7) & (g >= KEPT))

    doc_copy = pltpu.make_async_copy(doc_hbm, doc, d_sem)
    doc_copy.start()
    for g in range(GROUPS):
        for c in load(g):
            c.start()
    for g in range(GROUPS):
        load_q(g).start()

    barrier = pltpu.get_barrier_semaphore()

    @pl.when(has_prev)
    def _():
        pl.semaphore_signal(barrier, inc=1, device_id=at(before), device_id_type=MESH)

    @pl.when(is_middle)
    def _():
        pl.semaphore_signal(barrier, inc=1, device_id=at(jnp.maximum(b - 10, 0)), device_id_type=MESH)

    @pl.when(is_target)
    def _():
        pl.semaphore_signal(barrier, inc=1, device_id=at(jnp.minimum(b + 6, n - 1)), device_id_type=MESH)

    pl.semaphore_signal(barrier, inc=1, device_id=at(sibling), device_id_type=MESH)

    @pl.when(jnp.logical_not(has_two))
    def _():
        kv[:, 0] = jnp.zeros((GROUPS, 2 * TOK, HEAD), jnp.bfloat16)
        tag[0] = jnp.full((16, TOK), -1, jnp.bfloat16)

    @pl.when(jnp.logical_not(has_prev))
    def _():
        kv[:, 2] = jnp.zeros((GROUPS, 2 * TOK, HEAD), jnp.bfloat16)
        tag[2] = jnp.full((16, TOK), -1, jnp.bfloat16)

    doc_copy.wait()
    docs = jnp.broadcast_to(doc[...].reshape(1, TOK).astype(jnp.float32), (TOK, TOK))
    tag[OWN] = docs[:16].astype(jnp.bfloat16)
    column[...] = docs.T

    def when(condition, action):
        pl.when(condition)(action)

    pl.semaphore_wait(barrier, 1 + has_next.astype(jnp.int32) + (is_source | is_middle).astype(jnp.int32))
    when(has_next, lambda: move_tag(LINK).start())
    for g in range(GROUPS):
        for c in load(g):
            c.wait()
        if g < AHEAD:
            when(has_next, lambda: move(LINK, g).start())
    for m in range(DIVERT):
        when(is_source, lambda: to_middle(m).start())
    row = lax.broadcasted_iota(jnp.int32, (TOK, TOK), 0)
    col = lax.broadcasted_iota(jnp.int32, (TOK, TOK), 1)
    bias[:, OWN * TOK :] = jnp.where((column[...] == docs) & (col <= row), 0.0, MASKED)
    def step(it, _):
        @pl.when(it == 0)
        def _():
            when(has_prev, lambda: move_tag(LINK).wait_recv())
            when(has_prev & has_next, lambda: move_tag(RELAY).start())
            move_tag(PAIR_NEAR).start()
            when(core == 0, lambda: move_tag(PAIR_FAR).start())

        @pl.when(it < GROUPS)
        def _():
            when(has_prev, lambda: move(LINK, it).wait_recv())
            when(relays(it), lambda: move(RELAY, it).start())
            move(PAIR_NEAR, it).start()
            when(core == 0, lambda: move(PAIR_FAR, it).start())

        when(has_next & (it + AHEAD < GROUPS), lambda: move(LINK, it + AHEAD).start())

        @pl.when(is_middle & (it >= KEPT - 1) & (it < GROUPS - 1))
        def _():
            to_middle(it - KEPT + 1).wait_recv()
            from_middle(it - KEPT + 1).start()

        @pl.when(it == LAG)
        def _():
            when(has_two, lambda: move_tag(RELAY).wait_recv())
            when(core == 1, lambda: move_tag(PAIR_FAR).start())

        @pl.when((it >= LAG) & (it < GROUPS + LAG))
        def _():
            when(has_two, lambda: move(RELAY, it - LAG).wait_recv())
            when(core == 1, lambda: move(PAIR_FAR, it - LAG).start())

        @pl.when(it == LAG + 1)
        def _():
            move_tag(PAIR_NEAR).wait_recv()
            move_tag(PAIR_FAR).wait_recv()
            for s in range(OWN):
                other = jnp.broadcast_to(tag[s][:1].astype(jnp.float32), (TOK, TOK))
                bias[:, s * TOK : (s + 1) * TOK] = jnp.where(column[...] == other, 0.0, MASKED)

        @pl.when(it > LAG)
        def _():
            g = it - LAG - 1
            move(PAIR_NEAR, g).wait_recv()
            move(PAIR_FAR, g).wait_recv()
            load_q(g).wait()
            attend(qv.at[g], kv.at[g], bias, part.at[g])

        return 0

    lax.fori_loop(0, FIRST + LAG + 1, step, 0)

    for kind in routes:
        if kind == LINK:
            when(has_next, lambda: move_tag(LINK).wait_send())
        elif kind == RELAY:
            when(has_prev & has_next, lambda: move_tag(RELAY).wait_send())
        else:
            move_tag(kind).wait_send()

    def finish(g, _):
        when(has_next, lambda: move(LINK, g).wait_send())
        when(relays(g), lambda: move(RELAY, g).wait_send())
        move(PAIR_NEAR, g).wait_send()
        move(PAIR_FAR, g).wait_send()
        return 0

    lax.fori_loop(0, GROUPS, finish, 0)
    for m in range(DIVERT):
        when(is_source, lambda: to_middle(m).wait_send())
        when(is_middle, lambda: from_middle(m).wait_send())
    for g in range(FIRST, GROUPS):
        load_q(g).wait()
        move(PAIR_NEAR, g).wait_recv()
        move(PAIR_FAR, g).wait_recv()


def last_kernel(part, kv, qv, bias, o_hbm, out, sem):
    def store(g):
        source = part.at[g] if g < FIRST else out.at[g - FIRST]
        return pltpu.make_async_copy(source, o_hbm.at[:, group_columns(g)], sem.at[g])

    for g in range(FIRST):
        store(g).start()
    for g in range(FIRST, GROUPS):
        attend(qv.at[g], kv.at[g], bias, out.at[g - FIRST])
        store(g).start()
    for g in range(GROUPS):
        store(g).wait()


def solution(mesh):
    n, outer = mesh.size, mesh.shape["outer"]

    def local(queries, keys, values, documents):
        anywhere = pl.BlockSpec(memory_space=pl.ANY)
        vmem = pl.BlockSpec(memory_space=pltpu.VMEM)
        arguments = [pltpu.with_memory_space_constraint(x, pltpu.HBM) for x in (queries, keys, values, documents)]
        part, kv, qv, bias = pl.pallas_call(
            functools.partial(first_kernel, n, outer),
            out_shape=(
                pltpu.VMEM((FIRST, TOK, RATIO * HEAD), jnp.bfloat16),
                pltpu.VMEM((GROUPS, 5, 2 * TOK, HEAD), jnp.bfloat16),
                pltpu.VMEM((GROUPS, TOK, RATIO * HEAD), jnp.bfloat16),
                pltpu.VMEM((TOK, 5 * TOK), jnp.float32),
            ),
            in_specs=[anywhere] * 4,
            out_specs=(vmem,) * 4,
            scratch_shapes=[
                pltpu.VMEM((TOK,), jnp.int32),
                pltpu.VMEM((TOK, TOK), jnp.float32),
                pltpu.VMEM((5, 16, TOK), jnp.bfloat16),
                pltpu.VMEM((DIVERT, 2 * TOK, HEAD), jnp.bfloat16),
                pltpu.SemaphoreType.DMA((GROUPS, 2)),
                pltpu.SemaphoreType.DMA((GROUPS,)),
                pltpu.SemaphoreType.DMA,
                pltpu.SemaphoreType.DMA((4, GROUPS)),
                pltpu.SemaphoreType.DMA((4, GROUPS)),
                pltpu.SemaphoreType.DMA((4,)),
                pltpu.SemaphoreType.DMA((4,)),
                pltpu.SemaphoreType.DMA((2, DIVERT)),
                pltpu.SemaphoreType.DMA((DIVERT,)),
            ],
            name="relay_and_attend",
            compiler_params=pltpu.CompilerParams(
                collective_id=0, has_side_effects=True, vmem_limit_bytes=24 * 2**20
            ),
        )(*arguments)
        return pl.pallas_call(
            last_kernel,
            out_shape=jax.ShapeDtypeStruct(queries.shape, jnp.bfloat16),
            in_specs=[vmem] * 4,
            out_specs=anywhere,
            scratch_shapes=[
                pltpu.VMEM((GROUPS - FIRST, TOK, RATIO * HEAD), jnp.bfloat16),
                pltpu.SemaphoreType.DMA((GROUPS,)),
            ],
            name="attend_and_write",
            compiler_params=pltpu.CompilerParams(vmem_limit_bytes=24 * 2**20),
        )(part, kv, qv, bias)

    row = P(("inner", "outer"), None)
    return jax.shard_map(local, mesh=mesh, in_specs=(row, row, row, P(("inner", "outer"))), out_specs=row, check_vma=False)
```

```python
import functools

import jax
import jax.numpy as jnp
from jax import lax
from jax.experimental import pallas as pl
from jax.experimental.pallas import tpu as pltpu
from jax.sharding import PartitionSpec as P

MESH = pl.DeviceIdType.MESH
HEAD = 128
GROUPS = 8
RATIO = 8
TOK = 128
NEAR = 2
OWN = 4
AHEAD = 4
LAG = 3
DIVERT = 8
KEPT = GROUPS - DIVERT
FIRST = GROUPS - 1
MASKED = -1e30
LINK, RELAY, PAIR_NEAR, PAIR_FAR = range(4)
LOG2E = 1.4426950408889634


def group_columns(g):
    return pl.ds(pl.multiple_of(g * RATIO * HEAD, HEAD), RATIO * HEAD)


def scores(q_at, k, bias, h):
    q = q_at[:, h * HEAD : (h + 1) * HEAD]
    s = lax.dot_general(q, k, (((1,), (1,)), ((), ())), preferred_element_type=jnp.float32)
    return s * (HEAD**-0.5 * LOG2E) + bias


def keys_values(kv_at, first, last):
    k = kv_at[first:last, :TOK, :].reshape((last - first) * TOK, HEAD)
    v = kv_at[first:last, TOK:, :].reshape((last - first) * TOK, HEAD)
    return k, jnp.concatenate([v, jnp.ones_like(v)], axis=1)


def attend_near(q_at, kv_at, bias, acc_at, top_at):
    k, v = keys_values(kv_at, NEAR, OWN + 1)
    for h in range(RATIO):
        t = scores(q_at, k, bias[:, NEAR * TOK :], h)
        top = jnp.max(t, axis=-1, keepdims=True)
        p = jnp.exp2(t - top).astype(jnp.bfloat16)
        acc_at[h] = jnp.dot(p, v, preferred_element_type=jnp.float32)
        top_at[h] = jnp.broadcast_to(top, (TOK, HEAD))


def attend_far(q_at, kv_at, bias, acc_at, top_at, out_at):
    k, v = keys_values(kv_at, 0, NEAR)
    for h in range(RATIO):
        t = scores(q_at, k, bias[:, : NEAR * TOK], h)
        old = top_at[h]
        top = jnp.maximum(old, jnp.max(t, axis=-1, keepdims=True))
        p = jnp.exp2(t - jnp.concatenate([top, top], axis=1)).astype(jnp.bfloat16)
        fade = jnp.exp2(old - top)
        acc = acc_at[h] * jnp.concatenate([fade, fade], axis=1) + jnp.dot(p, v, preferred_element_type=jnp.float32)
        out_at[:, h * HEAD : (h + 1) * HEAD] = (acc[:, :HEAD] / acc[:, HEAD:]).astype(jnp.bfloat16)


def first_kernel(n, outer, q_hbm, k_hbm, v_hbm, doc_hbm, part, kv, qv, bias, acc, top, doc, column, tag, mid, in_sem, q_sem, d_sem, send, recv, tsend, trecv, dsend, drecv):
    b = lax.axis_index("inner") * outer + lax.axis_index("outer")
    core = lax.rem(b, 2)
    sibling = b + 1 - 2 * core
    has_next = b < n - 2
    has_prev = b >= 2
    has_two = b >= 4
    z = lax.rem(b // 2, 8)
    more_rows = b < n - 16
    ahead = AHEAD + 2 * ((7 - z) // 7)
    is_source = (z == 6) & more_rows
    is_middle = (z == 3) & (b >= 16)
    is_target = (z == 0) & (b >= 16)
    after = jnp.minimum(b + 2, n - 2 + core)
    before = jnp.maximum(b - 2, core)

    def at(device):
        return (device // outer, lax.rem(device, outer))

    def load(g):
        cols = pl.ds(pl.multiple_of(g * HEAD, HEAD), HEAD)
        return (
            pltpu.make_async_copy(k_hbm.at[:, cols], kv.at[g, OWN, pl.ds(0, TOK)], in_sem.at[g, 0]),
            pltpu.make_async_copy(v_hbm.at[:, cols], kv.at[g, OWN, pl.ds(TOK, TOK)], in_sem.at[g, 1]),
        )

    def load_q(g):
        return pltpu.make_async_copy(q_hbm.at[:, group_columns(g)], qv.at[g], q_sem.at[g])

    near_src = OWN - 2 * core
    far_src = 2 - 2 * core
    routes = {
        LINK: (OWN, 2, after),
        RELAY: (2, 0, after),
        PAIR_NEAR: (near_src, 3, sibling),
        PAIR_FAR: (far_src, 1, sibling),
    }

    def move(kind, g):
        src, dst, device = routes[kind]
        return pltpu.make_async_remote_copy(
            src_ref=kv.at[g, src],
            dst_ref=kv.at[g, dst],
            send_sem=send.at[kind, g],
            recv_sem=recv.at[kind, g],
            device_id=at(device),
            device_id_type=MESH,
        )

    def move_tag(kind):
        src, dst, device = routes[kind]
        return pltpu.make_async_remote_copy(
            src_ref=tag.at[src],
            dst_ref=tag.at[dst],
            send_sem=tsend.at[kind],
            recv_sem=trecv.at[kind],
            device_id=at(device),
            device_id_type=MESH,
        )

    def to_middle(m):
        return pltpu.make_async_remote_copy(
            src_ref=kv.at[KEPT + m, OWN],
            dst_ref=mid.at[m],
            send_sem=dsend.at[0, m],
            recv_sem=drecv.at[m],
            device_id=at(jnp.minimum(b + 10, n - 1)),
            device_id_type=MESH,
        )

    def from_middle(m):
        return pltpu.make_async_remote_copy(
            src_ref=mid.at[m],
            dst_ref=kv.at[KEPT + m, 0],
            send_sem=dsend.at[1, m],
            recv_sem=recv.at[RELAY, KEPT + m],
            device_id=at(jnp.maximum(b - 6, 0)),
            device_id_type=MESH,
        )

    def relays(g):
        return has_prev & has_next & jnp.logical_not((z == 7) & (g >= KEPT))

    doc_copy = pltpu.make_async_copy(doc_hbm, doc, d_sem)
    doc_copy.start()
    for g in range(GROUPS):
        for c in load(g):
            c.start()
    for g in range(GROUPS):
        load_q(g).start()

    barrier = pltpu.get_barrier_semaphore()

    @pl.when(has_prev)
    def _():
        pl.semaphore_signal(barrier, inc=1, device_id=at(before), device_id_type=MESH)

    @pl.when(is_middle)
    def _():
        pl.semaphore_signal(barrier, inc=1, device_id=at(jnp.maximum(b - 10, 0)), device_id_type=MESH)

    @pl.when(is_target)
    def _():
        pl.semaphore_signal(barrier, inc=1, device_id=at(jnp.minimum(b + 6, n - 1)), device_id_type=MESH)

    pl.semaphore_signal(barrier, inc=1, device_id=at(sibling), device_id_type=MESH)

    @pl.when(jnp.logical_not(has_two))
    def _():
        kv[:, 0] = jnp.zeros((GROUPS, 2 * TOK, HEAD), jnp.bfloat16)
        tag[0] = jnp.full((16, TOK), -1, jnp.bfloat16)

    @pl.when(jnp.logical_not(has_prev))
    def _():
        kv[:, 2] = jnp.zeros((GROUPS, 2 * TOK, HEAD), jnp.bfloat16)
        tag[2] = jnp.full((16, TOK), -1, jnp.bfloat16)

    doc_copy.wait()
    docs = jnp.broadcast_to(doc[...].reshape(1, TOK).astype(jnp.float32), (TOK, TOK))
    tag[OWN] = docs[:16].astype(jnp.bfloat16)
    column[...] = docs.T

    def when(condition, action):
        pl.when(condition)(action)

    pl.semaphore_wait(barrier, 1 + has_next.astype(jnp.int32) + (is_source | is_middle).astype(jnp.int32))
    when(has_next, lambda: move_tag(LINK).start())
    for g in range(GROUPS):
        for c in load(g):
            c.wait()
        if g < AHEAD + 2:
            when(has_next & (g < ahead), lambda: move(LINK, g).start())
    for m in range(DIVERT):
        when(is_source, lambda: to_middle(m).start())
    row = lax.broadcasted_iota(jnp.int32, (TOK, TOK), 0)
    col = lax.broadcasted_iota(jnp.int32, (TOK, TOK), 1)
    bias[:, OWN * TOK :] = jnp.where((column[...] == docs) & (col <= row), 0.0, MASKED)
    def mask(s):
        other = jnp.broadcast_to(tag[s][:1].astype(jnp.float32), (TOK, TOK))
        bias[:, s * TOK : (s + 1) * TOK] = jnp.where(column[...] == other, 0.0, MASKED)

    def step(it, _):
        @pl.when(it == 0)
        def _():
            when(has_prev, lambda: move_tag(LINK).wait_recv())
            when(has_prev & has_next, lambda: move_tag(RELAY).start())
            move_tag(PAIR_NEAR).start()
            when(core == 0, lambda: move_tag(PAIR_FAR).start())

        @pl.when(it < GROUPS)
        def _():
            when(has_prev, lambda: move(LINK, it).wait_recv())
            when(relays(it), lambda: move(RELAY, it).start())
            move(PAIR_NEAR, it).start()
            when(core == 0, lambda: move(PAIR_FAR, it).start())

        when(has_next & (it + ahead < GROUPS), lambda: move(LINK, it + ahead).start())

        @pl.when(is_middle & (it < GROUPS))
        def _():
            to_middle(it).wait_recv()
            from_middle(it).start()

        @pl.when(it == 1)
        def _():
            move_tag(PAIR_NEAR).wait_recv()
            mask(2)
            mask(3)

        @pl.when((it >= 1) & (it < GROUPS + 1))
        def _():
            g = it - 1
            move(PAIR_NEAR, g).wait_recv()
            load_q(g).wait()
            attend_near(qv.at[g], kv.at[g], bias, acc.at[g], top.at[g])

        @pl.when(it == LAG)
        def _():
            when(has_two, lambda: move_tag(RELAY).wait_recv())
            when(core == 1, lambda: move_tag(PAIR_FAR).start())

        @pl.when((it >= LAG) & (it < GROUPS + LAG))
        def _():
            when(has_two, lambda: move(RELAY, it - LAG).wait_recv())
            when(core == 1, lambda: move(PAIR_FAR, it - LAG).start())

        @pl.when(it == LAG + 1)
        def _():
            move_tag(PAIR_FAR).wait_recv()
            mask(0)
            mask(1)

        @pl.when(it > LAG)
        def _():
            g = it - LAG - 1
            move(PAIR_FAR, g).wait_recv()
            attend_far(qv.at[g], kv.at[g], bias, acc.at[g], top.at[g], part.at[g])

        return 0

    lax.fori_loop(0, FIRST + LAG + 1, step, 0)

    for kind in routes:
        if kind == LINK:
            when(has_next, lambda: move_tag(LINK).wait_send())
        elif kind == RELAY:
            when(has_prev & has_next, lambda: move_tag(RELAY).wait_send())
        else:
            move_tag(kind).wait_send()

    def finish(g, _):
        when(has_next, lambda: move(LINK, g).wait_send())
        when(relays(g), lambda: move(RELAY, g).wait_send())
        move(PAIR_NEAR, g).wait_send()
        move(PAIR_FAR, g).wait_send()
        return 0

    lax.fori_loop(0, GROUPS, finish, 0)
    for m in range(DIVERT):
        when(is_source, lambda: to_middle(m).wait_send())
        when(is_middle, lambda: from_middle(m).wait_send())
    for g in range(FIRST, GROUPS):
        move(PAIR_FAR, g).wait_recv()


def last_kernel(part, kv, qv, bias, acc, top, o_hbm, out, sem):
    def store(g):
        source = part.at[g] if g < FIRST else out.at[g - FIRST]
        return pltpu.make_async_copy(source, o_hbm.at[:, group_columns(g)], sem.at[g])

    for g in range(FIRST):
        store(g).start()
    for g in range(FIRST, GROUPS):
        attend_far(qv.at[g], kv.at[g], bias, acc.at[g], top.at[g], out.at[g - FIRST])
        store(g).start()
    for g in range(GROUPS):
        store(g).wait()


def solution(mesh):
    n, outer = mesh.size, mesh.shape["outer"]

    def local(queries, keys, values, documents):
        anywhere = pl.BlockSpec(memory_space=pl.ANY)
        vmem = pl.BlockSpec(memory_space=pltpu.VMEM)
        arguments = [pltpu.with_memory_space_constraint(x, pltpu.HBM) for x in (queries, keys, values, documents)]
        handed = pl.pallas_call(
            functools.partial(first_kernel, n, outer),
            out_shape=(
                pltpu.VMEM((FIRST, TOK, RATIO * HEAD), jnp.bfloat16),
                pltpu.VMEM((GROUPS, 5, 2 * TOK, HEAD), jnp.bfloat16),
                pltpu.VMEM((GROUPS, TOK, RATIO * HEAD), jnp.bfloat16),
                pltpu.VMEM((TOK, 5 * TOK), jnp.float32),
                pltpu.VMEM((GROUPS, RATIO, TOK, 2 * HEAD), jnp.float32),
                pltpu.VMEM((GROUPS, RATIO, TOK, HEAD), jnp.float32),
            ),
            in_specs=[anywhere] * 4,
            out_specs=(vmem,) * 6,
            scratch_shapes=[
                pltpu.VMEM((TOK,), jnp.int32),
                pltpu.VMEM((TOK, TOK), jnp.float32),
                pltpu.VMEM((5, 16, TOK), jnp.bfloat16),
                pltpu.VMEM((DIVERT, 2 * TOK, HEAD), jnp.bfloat16),
                pltpu.SemaphoreType.DMA((GROUPS, 2)),
                pltpu.SemaphoreType.DMA((GROUPS,)),
                pltpu.SemaphoreType.DMA,
                pltpu.SemaphoreType.DMA((4, GROUPS)),
                pltpu.SemaphoreType.DMA((4, GROUPS)),
                pltpu.SemaphoreType.DMA((4,)),
                pltpu.SemaphoreType.DMA((4,)),
                pltpu.SemaphoreType.DMA((2, DIVERT)),
                pltpu.SemaphoreType.DMA((DIVERT,)),
            ],
            name="relay_and_attend",
            compiler_params=pltpu.CompilerParams(
                collective_id=0, has_side_effects=True, vmem_limit_bytes=16 * 2**20
            ),
        )(*arguments)
        return pl.pallas_call(
            last_kernel,
            out_shape=jax.ShapeDtypeStruct(queries.shape, jnp.bfloat16),
            in_specs=[vmem] * 6,
            out_specs=anywhere,
            scratch_shapes=[
                pltpu.VMEM((GROUPS - FIRST, TOK, RATIO * HEAD), jnp.bfloat16),
                pltpu.SemaphoreType.DMA((GROUPS,)),
            ],
            name="attend_and_write",
            compiler_params=pltpu.CompilerParams(vmem_limit_bytes=16 * 2**20),
        )(*handed)

    row = P(("inner", "outer"), None)
    return jax.shard_map(local, mesh=mesh, in_specs=(row, row, row, P(("inner", "outer"))), out_specs=row, check_vma=False)
```

```python
import functools

import jax
import jax.numpy as jnp
from jax import lax
from jax.experimental import pallas as pl
from jax.experimental.pallas import tpu as pltpu
from jax.sharding import PartitionSpec as P

MESH = pl.DeviceIdType.MESH
HEAD = 128
GROUPS = 8
RATIO = 8
TOK = 128
NEAR = 2
OWN = 4
AHEAD = 4
LAG = 3
DIVERT = 8
KEPT = GROUPS - DIVERT
FIRST = GROUPS - 1
MASKED = -1e30
LINK, RELAY, PAIR_NEAR, PAIR_FAR = range(4)
LOG2E = 1.4426950408889634


def group_columns(g):
    return pl.ds(pl.multiple_of(g * RATIO * HEAD, HEAD), RATIO * HEAD)


BATCH = 4


def scores(q_at, k, bias, h):
    q, g = q_at
    q = [q[:, pl.ds(pl.multiple_of((g * RATIO + h + i) * HEAD, HEAD), HEAD)] for i in range(BATCH)]
    s = lax.dot_general(
        jnp.concatenate(q, axis=0), k, (((1,), (1,)), ((), ())), preferred_element_type=jnp.float32
    )
    t = (s * (HEAD**-0.5 * LOG2E)).reshape(BATCH, TOK, -1) + bias[None]
    return t.reshape(BATCH * TOK, -1)


def keys_values(kv_at, first, last):
    k = kv_at[first:last, :TOK, :].reshape((last - first) * TOK, HEAD)
    v = kv_at[first:last, TOK:, :].reshape((last - first) * TOK, HEAD)
    return k, jnp.concatenate([v, jnp.ones_like(v)], axis=1)


def attend_near(q_at, kv_at, bias, acc_at, top_at):
    k, v = keys_values(kv_at, NEAR, OWN + 1)
    for h in range(0, RATIO, BATCH):
        t = scores(q_at, k, bias[:, NEAR * TOK :], h)
        top = jnp.max(t, axis=-1, keepdims=True)
        p = jnp.exp2(t - top).astype(jnp.bfloat16)
        acc_at[h : h + BATCH] = jnp.dot(p, v, preferred_element_type=jnp.float32).reshape(BATCH, TOK, 2 * HEAD)
        top_at[h : h + BATCH] = jnp.broadcast_to(top, (BATCH * TOK, HEAD)).reshape(BATCH, TOK, HEAD)


def attend_far(q_at, kv_at, bias, acc_at, top_at, out_at):
    k, v = keys_values(kv_at, 0, NEAR)
    for h in range(0, RATIO, BATCH):
        t = scores(q_at, k, bias[:, : NEAR * TOK], h)
        old = top_at[h : h + BATCH].reshape(BATCH * TOK, HEAD)
        top = jnp.maximum(old, jnp.max(t, axis=-1, keepdims=True))
        p = jnp.exp2(t - jnp.concatenate([top, top], axis=1)).astype(jnp.bfloat16)
        fade = jnp.exp2(old - top)
        acc = acc_at[h : h + BATCH].reshape(BATCH * TOK, 2 * HEAD) * jnp.concatenate([fade, fade], axis=1)
        acc = acc + jnp.dot(p, v, preferred_element_type=jnp.float32)
        out = (acc[:, :HEAD] / acc[:, HEAD:]).astype(jnp.bfloat16)
        for i in range(BATCH):
            out_at[:, (h + i) * HEAD : (h + i + 1) * HEAD] = out[i * TOK : (i + 1) * TOK]


def first_kernel(n, outer, q_hbm, k_hbm, v_hbm, doc_hbm, part, kv, qv, bias, acc, top, kv_in, doc, column, tag, mid, in_sem, q_sem, d_sem, send, recv, tsend, trecv, dsend, drecv):
    b = lax.axis_index("inner") * outer + lax.axis_index("outer")
    core = lax.rem(b, 2)
    sibling = b + 1 - 2 * core
    has_next = b < n - 2
    has_prev = b >= 2
    has_two = b >= 4
    z = lax.rem(b // 2, 8)
    more_rows = b < n - 16
    ahead = AHEAD + 2 * ((7 - z) // 7)
    is_source = (z == 6) & more_rows
    is_middle = (z == 3) & (b >= 16)
    is_target = (z == 0) & (b >= 16)
    after = jnp.minimum(b + 2, n - 2 + core)
    before = jnp.maximum(b - 2, core)

    def at(device):
        return (device // outer, lax.rem(device, outer))

    load_q = pltpu.make_async_copy(q_hbm, qv, q_sem)
    load_k = pltpu.make_async_copy(k_hbm, kv_in.at[0], in_sem.at[0])
    load_v = pltpu.make_async_copy(v_hbm, kv_in.at[1], in_sem.at[1])

    near_src = OWN - 2 * core
    far_src = 2 - 2 * core
    routes = {
        LINK: (OWN, 2, after),
        RELAY: (2, 0, after),
        PAIR_NEAR: (near_src, 3, sibling),
        PAIR_FAR: (far_src, 1, sibling),
    }

    def move(kind, g):
        src, dst, device = routes[kind]
        return pltpu.make_async_remote_copy(
            src_ref=kv.at[g, src],
            dst_ref=kv.at[g, dst],
            send_sem=send.at[kind, g],
            recv_sem=recv.at[kind, g],
            device_id=at(device),
            device_id_type=MESH,
        )

    def move_tag(kind):
        src, dst, device = routes[kind]
        return pltpu.make_async_remote_copy(
            src_ref=tag.at[src],
            dst_ref=tag.at[dst],
            send_sem=tsend.at[kind],
            recv_sem=trecv.at[kind],
            device_id=at(device),
            device_id_type=MESH,
        )

    def to_middle(m):
        return pltpu.make_async_remote_copy(
            src_ref=kv.at[KEPT + m, OWN],
            dst_ref=mid.at[m],
            send_sem=dsend.at[0, m],
            recv_sem=drecv.at[m],
            device_id=at(jnp.minimum(b + 10, n - 1)),
            device_id_type=MESH,
        )

    def from_middle(m):
        return pltpu.make_async_remote_copy(
            src_ref=mid.at[m],
            dst_ref=kv.at[KEPT + m, 0],
            send_sem=dsend.at[1, m],
            recv_sem=recv.at[RELAY, KEPT + m],
            device_id=at(jnp.maximum(b - 6, 0)),
            device_id_type=MESH,
        )

    def relays(g):
        return has_prev & has_next & jnp.logical_not((z == 7) & (g >= KEPT))

    barrier = pltpu.get_barrier_semaphore()

    @pl.when(has_prev)
    def _():
        pl.semaphore_signal(barrier, inc=1, device_id=at(before), device_id_type=MESH)

    @pl.when(is_middle)
    def _():
        pl.semaphore_signal(barrier, inc=1, device_id=at(jnp.maximum(b - 10, 0)), device_id_type=MESH)

    @pl.when(is_target)
    def _():
        pl.semaphore_signal(barrier, inc=1, device_id=at(jnp.minimum(b + 6, n - 1)), device_id_type=MESH)

    pl.semaphore_signal(barrier, inc=1, device_id=at(sibling), device_id_type=MESH)

    doc_copy = pltpu.make_async_copy(doc_hbm, doc, d_sem)
    load_k.start()
    load_v.start()
    doc_copy.start()
    load_q.start()

    @pl.when(jnp.logical_not(has_two))
    def _():
        kv[:, 0] = jnp.zeros((GROUPS, 2 * TOK, HEAD), jnp.bfloat16)
        tag[0] = jnp.full((16, TOK), -1, jnp.bfloat16)

    @pl.when(jnp.logical_not(has_prev))
    def _():
        kv[:, 2] = jnp.zeros((GROUPS, 2 * TOK, HEAD), jnp.bfloat16)
        tag[2] = jnp.full((16, TOK), -1, jnp.bfloat16)

    def when(condition, action):
        pl.when(condition)(action)

    pl.semaphore_wait(barrier, 1 + has_next.astype(jnp.int32) + (is_source | is_middle).astype(jnp.int32))
    load_k.wait()
    load_v.wait()
    for g in range(GROUPS):
        for i in range(2):
            kv[g, OWN, i * TOK : (i + 1) * TOK] = kv_in[i, :, g * HEAD : (g + 1) * HEAD]
        if g < AHEAD + 2:
            when(has_next & (g < ahead), lambda: move(LINK, g).start())
        if g == 0:
            doc_copy.wait()
            docs = jnp.broadcast_to(doc[...].reshape(1, TOK).astype(jnp.float32), (TOK, TOK))
            tag[OWN] = docs[:16].astype(jnp.bfloat16)
            when(has_next, lambda: move_tag(LINK).start())
    for m in range(DIVERT):
        when(is_source, lambda: to_middle(m).start())
    column[...] = docs.T
    row = lax.broadcasted_iota(jnp.int32, (TOK, TOK), 0)
    col = lax.broadcasted_iota(jnp.int32, (TOK, TOK), 1)
    bias[:, OWN * TOK :] = jnp.where((column[...] == docs) & (col <= row), 0.0, MASKED)
    def mask(s):
        other = jnp.broadcast_to(tag[s][:1].astype(jnp.float32), (TOK, TOK))
        bias[:, s * TOK : (s + 1) * TOK] = jnp.where(column[...] == other, 0.0, MASKED)

    def step(it, _):
        @pl.when(it == 0)
        def _():
            when(has_prev, lambda: move_tag(LINK).wait_recv())
            when(has_prev & has_next, lambda: move_tag(RELAY).start())
            move_tag(PAIR_NEAR).start()
            when(core == 0, lambda: move_tag(PAIR_FAR).start())

        @pl.when(it < GROUPS)
        def _():
            when(has_prev, lambda: move(LINK, it).wait_recv())
            when(relays(it), lambda: move(RELAY, it).start())
            move(PAIR_NEAR, it).start()
            when(core == 0, lambda: move(PAIR_FAR, it).start())

        when(has_next & (it + ahead < GROUPS), lambda: move(LINK, it + ahead).start())

        def pass_on(m):
            to_middle(m).wait_recv()
            from_middle(m).start()

        @pl.when(is_middle & (it >= 1) & (it < 7))
        def _():
            m = it - 1 + (it // 5)
            pass_on(m)
            when((it == 4) | (it == 6), lambda: pass_on(m + 1))

        @pl.when(it == 1)
        def _():
            load_q.wait()
            move_tag(PAIR_NEAR).wait_recv()
            mask(2)
            mask(3)

        @pl.when((it >= 1) & (it < GROUPS + 1))
        def _():
            g = it - 1
            move(PAIR_NEAR, g).wait_recv()
            attend_near((qv, g), kv.at[g], bias, acc.at[g], top.at[g])

        @pl.when(it == LAG)
        def _():
            when(has_two, lambda: move_tag(RELAY).wait_recv())
            when(core == 1, lambda: move_tag(PAIR_FAR).start())

        @pl.when((it >= LAG) & (it < GROUPS + LAG))
        def _():
            when(has_two, lambda: move(RELAY, it - LAG).wait_recv())
            when(core == 1, lambda: move(PAIR_FAR, it - LAG).start())

        @pl.when(it == LAG + 1)
        def _():
            move_tag(PAIR_FAR).wait_recv()
            mask(0)
            mask(1)

        @pl.when(it > LAG)
        def _():
            g = it - LAG - 1
            move(PAIR_FAR, g).wait_recv()
            attend_far((qv, g), kv.at[g], bias, acc.at[g], top.at[g], part.at[g])

        return 0

    lax.fori_loop(0, FIRST + LAG + 1, step, 0)

    for kind in routes:
        if kind == LINK:
            when(has_next, lambda: move_tag(LINK).wait_send())
        elif kind == RELAY:
            when(has_prev & has_next, lambda: move_tag(RELAY).wait_send())
        else:
            move_tag(kind).wait_send()

    def finish(g, _):
        when(has_next, lambda: move(LINK, g).wait_send())
        when(relays(g), lambda: move(RELAY, g).wait_send())
        move(PAIR_NEAR, g).wait_send()
        move(PAIR_FAR, g).wait_send()
        return 0

    lax.fori_loop(0, GROUPS, finish, 0)
    for m in range(DIVERT):
        when(is_source, lambda: to_middle(m).wait_send())
        when(is_middle, lambda: from_middle(m).wait_send())
    for g in range(FIRST, GROUPS):
        move(PAIR_FAR, g).wait_recv()


def last_kernel(part, kv, qv, bias, acc, top, o_hbm, out, sem):
    def store(g):
        source = part.at[g] if g < FIRST else out.at[g - FIRST]
        return pltpu.make_async_copy(source, o_hbm.at[:, group_columns(g)], sem.at[g])

    for g in range(FIRST):
        store(g).start()
    for g in range(FIRST, GROUPS):
        attend_far((qv, g), kv.at[g], bias, acc.at[g], top.at[g], out.at[g - FIRST])
        store(g).start()
    for g in range(GROUPS):
        store(g).wait()


def solution(mesh):
    n, outer = mesh.size, mesh.shape["outer"]

    def local(queries, keys, values, documents):
        anywhere = pl.BlockSpec(memory_space=pl.ANY)
        vmem = pl.BlockSpec(memory_space=pltpu.VMEM)
        arguments = [pltpu.with_memory_space_constraint(x, pltpu.HBM) for x in (queries, keys, values, documents)]
        handed = pl.pallas_call(
            functools.partial(first_kernel, n, outer),
            out_shape=(
                pltpu.VMEM((FIRST, TOK, RATIO * HEAD), jnp.bfloat16),
                pltpu.VMEM((GROUPS, 5, 2 * TOK, HEAD), jnp.bfloat16),
                pltpu.VMEM(queries.shape, jnp.bfloat16),
                pltpu.VMEM((TOK, 5 * TOK), jnp.float32),
                pltpu.VMEM((GROUPS, RATIO, TOK, 2 * HEAD), jnp.float32),
                pltpu.VMEM((GROUPS, RATIO, TOK, HEAD), jnp.float32),
            ),
            in_specs=[anywhere] * 4,
            out_specs=(vmem,) * 6,
            scratch_shapes=[
                pltpu.VMEM((2, TOK, GROUPS * HEAD), jnp.bfloat16),
                pltpu.VMEM((TOK,), jnp.int32),
                pltpu.VMEM((TOK, TOK), jnp.float32),
                pltpu.VMEM((5, 16, TOK), jnp.bfloat16),
                pltpu.VMEM((DIVERT, 2 * TOK, HEAD), jnp.bfloat16),
                pltpu.SemaphoreType.DMA((2,)),
                pltpu.SemaphoreType.DMA,
                pltpu.SemaphoreType.DMA,
                pltpu.SemaphoreType.DMA((4, GROUPS)),
                pltpu.SemaphoreType.DMA((4, GROUPS)),
                pltpu.SemaphoreType.DMA((4,)),
                pltpu.SemaphoreType.DMA((4,)),
                pltpu.SemaphoreType.DMA((2, DIVERT)),
                pltpu.SemaphoreType.DMA((DIVERT,)),
            ],
            name="relay_and_attend",
            compiler_params=pltpu.CompilerParams(
                collective_id=0, has_side_effects=True, vmem_limit_bytes=16 * 2**20
            ),
        )(*arguments)
        return pl.pallas_call(
            last_kernel,
            out_shape=jax.ShapeDtypeStruct(queries.shape, jnp.bfloat16),
            in_specs=[vmem] * 6,
            out_specs=anywhere,
            scratch_shapes=[
                pltpu.VMEM((GROUPS - FIRST, TOK, RATIO * HEAD), jnp.bfloat16),
                pltpu.SemaphoreType.DMA((GROUPS,)),
            ],
            name="attend_and_write",
            compiler_params=pltpu.CompilerParams(vmem_limit_bytes=16 * 2**20),
        )(*handed)

    row = P(("inner", "outer"), None)
    return jax.shard_map(local, mesh=mesh, in_specs=(row, row, row, P(("inner", "outer"))), out_specs=row, check_vma=False)
```

```python
import functools

import jax
import jax.numpy as jnp
from jax import lax
from jax.experimental import pallas as pl
from jax.experimental.pallas import tpu as pltpu
from jax.sharding import PartitionSpec as P

MESH = pl.DeviceIdType.MESH
HEAD = 128
GROUPS = 8
RATIO = 8
TOK = 128
NEAR = 2
OWN = 4
AHEAD = 4
LAG = 3
DIVERT = 8
KEPT = GROUPS - DIVERT
FIRST = GROUPS - 1
MASKED = -1e30
LINK, RELAY, PAIR_NEAR, PAIR_FAR = range(4)
LOG2E = 1.4426950408889634


def group_columns(g):
    return pl.ds(pl.multiple_of(g * RATIO * HEAD, HEAD), RATIO * HEAD)


NEAR_BATCH, FAR_BATCH = 8, 2


def scores(q_at, k, bias, h, batch):
    q, g = q_at
    q = [q[:, pl.ds(pl.multiple_of((g * RATIO + h + i) * HEAD, HEAD), HEAD)] for i in range(batch)]
    s = lax.dot_general(
        jnp.concatenate(q, axis=0), k, (((1,), (1,)), ((), ())), preferred_element_type=jnp.float32
    )
    t = (s * (HEAD**-0.5 * LOG2E)).reshape(batch, TOK, -1) + bias[None]
    return t.reshape(batch * TOK, -1)


def keys_values(kv_at, first, last):
    k = kv_at[first:last, :TOK, :].reshape((last - first) * TOK, HEAD)
    v = kv_at[first:last, TOK:, :].reshape((last - first) * TOK, HEAD)
    return k, v


def attend_near(q_at, kv_at, bias, acc_at, top_at):
    k, v = keys_values(kv_at, NEAR, OWN + 1)
    for h in range(0, RATIO, NEAR_BATCH):
        t = scores(q_at, k, bias[:, NEAR * TOK :], h, NEAR_BATCH)
        top = jnp.max(t, axis=-1, keepdims=True)
        p = jnp.exp2(t - top)
        total = jnp.broadcast_to(jnp.sum(p, axis=-1, keepdims=True), (NEAR_BATCH * TOK, HEAD))
        acc = jnp.concatenate([jnp.dot(p.astype(jnp.bfloat16), v, preferred_element_type=jnp.float32), total], axis=1)
        acc_at[h : h + NEAR_BATCH] = acc.reshape(NEAR_BATCH, TOK, 2 * HEAD)
        top_at[h : h + NEAR_BATCH] = jnp.broadcast_to(top, (NEAR_BATCH * TOK, HEAD)).reshape(NEAR_BATCH, TOK, HEAD)


def attend_far(q_at, kv_at, bias, acc_at, top_at, out_at):
    k, v = keys_values(kv_at, 0, NEAR)
    v = jnp.concatenate([v, jnp.ones_like(v)], axis=1)
    for h in range(0, RATIO, FAR_BATCH):
        t = scores(q_at, k, bias[:, : NEAR * TOK], h, FAR_BATCH)
        old = top_at[h : h + FAR_BATCH].reshape(FAR_BATCH * TOK, HEAD)
        top = jnp.maximum(old, jnp.max(t, axis=-1, keepdims=True))
        p = jnp.exp2(t - jnp.concatenate([top, top], axis=1)).astype(jnp.bfloat16)
        fade = jnp.exp2(old - top)
        acc = acc_at[h : h + FAR_BATCH].reshape(FAR_BATCH * TOK, 2 * HEAD) * jnp.concatenate([fade, fade], axis=1)
        acc = acc + jnp.dot(p, v, preferred_element_type=jnp.float32)
        out = (acc[:, :HEAD] / acc[:, HEAD:]).astype(jnp.bfloat16)
        for i in range(FAR_BATCH):
            out_at[:, (h + i) * HEAD : (h + i + 1) * HEAD] = out[i * TOK : (i + 1) * TOK]


def first_kernel(n, outer, q_hbm, k_hbm, v_hbm, doc_hbm, part, kv, qv, bias, acc, top, kv_in, doc, column, tag, mid, in_sem, q_sem, d_sem, send, recv, tsend, trecv, dsend, drecv):
    b = lax.axis_index("inner") * outer + lax.axis_index("outer")
    core = lax.rem(b, 2)
    sibling = b + 1 - 2 * core
    has_next = b < n - 2
    has_prev = b >= 2
    has_two = b >= 4
    z = lax.rem(b // 2, 8)
    more_rows = b < n - 16
    ahead = AHEAD + 2 * ((7 - z) // 7)
    is_source = (z == 6) & more_rows
    is_middle = (z == 3) & (b >= 16)
    is_target = (z == 0) & (b >= 16)
    after = jnp.minimum(b + 2, n - 2 + core)
    before = jnp.maximum(b - 2, core)

    def at(device):
        return (device // outer, lax.rem(device, outer))

    load_q = pltpu.make_async_copy(q_hbm, qv, q_sem)
    load_k = pltpu.make_async_copy(k_hbm, kv_in.at[0], in_sem.at[0])
    load_v = pltpu.make_async_copy(v_hbm, kv_in.at[1], in_sem.at[1])

    near_src = OWN - 2 * core
    far_src = 2 - 2 * core
    routes = {
        LINK: (OWN, 2, after),
        RELAY: (2, 0, after),
        PAIR_NEAR: (near_src, 3, sibling),
        PAIR_FAR: (far_src, 1, sibling),
    }

    def move(kind, g):
        src, dst, device = routes[kind]
        return pltpu.make_async_remote_copy(
            src_ref=kv.at[g, src],
            dst_ref=kv.at[g, dst],
            send_sem=send.at[kind, g],
            recv_sem=recv.at[kind, g],
            device_id=at(device),
            device_id_type=MESH,
        )

    def move_tag(kind):
        src, dst, device = routes[kind]
        return pltpu.make_async_remote_copy(
            src_ref=tag.at[src],
            dst_ref=tag.at[dst],
            send_sem=tsend.at[kind],
            recv_sem=trecv.at[kind],
            device_id=at(device),
            device_id_type=MESH,
        )

    def to_middle(m):
        return pltpu.make_async_remote_copy(
            src_ref=kv.at[KEPT + m, OWN],
            dst_ref=mid.at[m],
            send_sem=dsend.at[0, m],
            recv_sem=drecv.at[m],
            device_id=at(jnp.minimum(b + 10, n - 1)),
            device_id_type=MESH,
        )

    def from_middle(m):
        return pltpu.make_async_remote_copy(
            src_ref=mid.at[m],
            dst_ref=kv.at[KEPT + m, 0],
            send_sem=dsend.at[1, m],
            recv_sem=recv.at[RELAY, KEPT + m],
            device_id=at(jnp.maximum(b - 6, 0)),
            device_id_type=MESH,
        )

    def relays(g):
        return has_prev & has_next & jnp.logical_not((z == 7) & (g >= KEPT))

    barrier = pltpu.get_barrier_semaphore()

    @pl.when(has_prev)
    def _():
        pl.semaphore_signal(barrier, inc=1, device_id=at(before), device_id_type=MESH)

    @pl.when(is_middle)
    def _():
        pl.semaphore_signal(barrier, inc=1, device_id=at(jnp.maximum(b - 10, 0)), device_id_type=MESH)

    @pl.when(is_target)
    def _():
        pl.semaphore_signal(barrier, inc=1, device_id=at(jnp.minimum(b + 6, n - 1)), device_id_type=MESH)

    pl.semaphore_signal(barrier, inc=1, device_id=at(sibling), device_id_type=MESH)

    doc_copy = pltpu.make_async_copy(doc_hbm, doc, d_sem)
    load_k.start()
    load_v.start()
    doc_copy.start()
    load_q.start()

    @pl.when(jnp.logical_not(has_two))
    def _():
        kv[:, 0] = jnp.zeros((GROUPS, 2 * TOK, HEAD), jnp.bfloat16)
        tag[0] = jnp.full((16, TOK), -1, jnp.bfloat16)

    @pl.when(jnp.logical_not(has_prev))
    def _():
        kv[:, 2] = jnp.zeros((GROUPS, 2 * TOK, HEAD), jnp.bfloat16)
        tag[2] = jnp.full((16, TOK), -1, jnp.bfloat16)

    def when(condition, action):
        pl.when(condition)(action)

    pl.semaphore_wait(barrier, 1 + has_next.astype(jnp.int32) + (is_source | is_middle).astype(jnp.int32))
    load_k.wait()
    load_v.wait()
    for g in range(GROUPS):
        for i in range(2):
            kv[g, OWN, i * TOK : (i + 1) * TOK] = kv_in[i, :, g * HEAD : (g + 1) * HEAD]
        if g < AHEAD + 2:
            when(has_next & (g < ahead), lambda: move(LINK, g).start())
        when(is_source, lambda: to_middle(g).start())
        if g == 0:
            doc_copy.wait()
            docs = jnp.broadcast_to(doc[...].reshape(1, TOK).astype(jnp.float32), (TOK, TOK))
            tag[OWN] = docs[:16].astype(jnp.bfloat16)
            when(has_next, lambda: move_tag(LINK).start())
    column[...] = docs.T
    row = lax.broadcasted_iota(jnp.int32, (TOK, TOK), 0)
    col = lax.broadcasted_iota(jnp.int32, (TOK, TOK), 1)
    bias[:, OWN * TOK :] = jnp.where((column[...] == docs) & (col <= row), 0.0, MASKED)
    def mask(s):
        other = jnp.broadcast_to(tag[s][:1].astype(jnp.float32), (TOK, TOK))
        bias[:, s * TOK : (s + 1) * TOK] = jnp.where(column[...] == other, 0.0, MASKED)

    def step(it, _):
        @pl.when(it == 0)
        def _():
            when(has_prev, lambda: move_tag(LINK).wait_recv())
            when(has_prev & has_next, lambda: move_tag(RELAY).start())
            move_tag(PAIR_NEAR).start()
            when(core == 0, lambda: move_tag(PAIR_FAR).start())

        @pl.when(it < GROUPS)
        def _():
            when(has_prev, lambda: move(LINK, it).wait_recv())
            when(relays(it), lambda: move(RELAY, it).start())
            move(PAIR_NEAR, it).start()
            when(core == 0, lambda: move(PAIR_FAR, it).start())

        when(has_next & (it + ahead < GROUPS), lambda: move(LINK, it + ahead).start())

        def pass_on(m):
            to_middle(m).wait_recv()
            from_middle(m).start()

        @pl.when(is_middle & (it >= 1) & (it < 7))
        def _():
            m = it - 1 + (it // 5)
            pass_on(m)
            when((it == 4) | (it == 6), lambda: pass_on(m + 1))

        @pl.when(it == 1)
        def _():
            load_q.wait()
            move_tag(PAIR_NEAR).wait_recv()
            mask(2)
            mask(3)

        @pl.when((it >= 1) & (it < GROUPS + 1))
        def _():
            g = it - 1
            move(PAIR_NEAR, g).wait_recv()
            attend_near((qv, g), kv.at[g], bias, acc.at[g], top.at[g])

        @pl.when(it == LAG)
        def _():
            when(has_two, lambda: move_tag(RELAY).wait_recv())
            when(core == 1, lambda: move_tag(PAIR_FAR).start())

        @pl.when((it >= LAG) & (it < GROUPS + LAG))
        def _():
            when(has_two, lambda: move(RELAY, it - LAG).wait_recv())
            when(core == 1, lambda: move(PAIR_FAR, it - LAG).start())

        @pl.when(it == LAG + 1)
        def _():
            move_tag(PAIR_FAR).wait_recv()
            mask(0)
            mask(1)

        @pl.when((it > LAG) & (it < FIRST + LAG + 1))
        def _():
            g = it - LAG - 1
            move(PAIR_FAR, g).wait_recv()
            attend_far((qv, g), kv.at[g], bias, acc.at[g], top.at[g], part.at[g])

        return 0

    lax.fori_loop(0, FIRST + LAG + 1, step, 0)

    for kind in routes:
        if kind == LINK:
            when(has_next, lambda: move_tag(LINK).wait_send())
        elif kind == RELAY:
            when(has_prev & has_next, lambda: move_tag(RELAY).wait_send())
        else:
            move_tag(kind).wait_send()

    def finish(g, _):
        when(has_next, lambda: move(LINK, g).wait_send())
        when(relays(g), lambda: move(RELAY, g).wait_send())
        move(PAIR_NEAR, g).wait_send()
        move(PAIR_FAR, g).wait_send()
        return 0

    lax.fori_loop(0, GROUPS, finish, 0)
    for m in range(DIVERT):
        when(is_source, lambda: to_middle(m).wait_send())
        when(is_middle, lambda: from_middle(m).wait_send())
    for g in range(FIRST, GROUPS):
        move(PAIR_FAR, g).wait_recv()


def last_kernel(part, kv, qv, bias, acc, top, o_hbm, out, sem):
    def store(g):
        source = part.at[g] if g < FIRST else out.at[g - FIRST]
        return pltpu.make_async_copy(source, o_hbm.at[:, group_columns(g)], sem.at[g])

    for g in range(FIRST):
        store(g).start()
    for g in range(FIRST, GROUPS):
        attend_far((qv, g), kv.at[g], bias, acc.at[g], top.at[g], out.at[g - FIRST])
        store(g).start()
    for g in range(GROUPS):
        store(g).wait()


def solution(mesh):
    n, outer = mesh.size, mesh.shape["outer"]

    def local(queries, keys, values, documents):
        anywhere = pl.BlockSpec(memory_space=pl.ANY)
        vmem = pl.BlockSpec(memory_space=pltpu.VMEM)
        arguments = [pltpu.with_memory_space_constraint(x, pltpu.HBM) for x in (queries, keys, values, documents)]
        handed = pl.pallas_call(
            functools.partial(first_kernel, n, outer),
            out_shape=(
                pltpu.VMEM((FIRST, TOK, RATIO * HEAD), jnp.bfloat16),
                pltpu.VMEM((GROUPS, 5, 2 * TOK, HEAD), jnp.bfloat16),
                pltpu.VMEM(queries.shape, jnp.bfloat16),
                pltpu.VMEM((TOK, 5 * TOK), jnp.float32),
                pltpu.VMEM((GROUPS, RATIO, TOK, 2 * HEAD), jnp.float32),
                pltpu.VMEM((GROUPS, RATIO, TOK, HEAD), jnp.float32),
            ),
            in_specs=[anywhere] * 4,
            out_specs=(vmem,) * 6,
            scratch_shapes=[
                pltpu.VMEM((2, TOK, GROUPS * HEAD), jnp.bfloat16),
                pltpu.VMEM((TOK,), jnp.int32),
                pltpu.VMEM((TOK, TOK), jnp.float32),
                pltpu.VMEM((5, 16, TOK), jnp.bfloat16),
                pltpu.VMEM((DIVERT, 2 * TOK, HEAD), jnp.bfloat16),
                pltpu.SemaphoreType.DMA((2,)),
                pltpu.SemaphoreType.DMA,
                pltpu.SemaphoreType.DMA,
                pltpu.SemaphoreType.DMA((4, GROUPS)),
                pltpu.SemaphoreType.DMA((4, GROUPS)),
                pltpu.SemaphoreType.DMA((4,)),
                pltpu.SemaphoreType.DMA((4,)),
                pltpu.SemaphoreType.DMA((2, DIVERT)),
                pltpu.SemaphoreType.DMA((DIVERT,)),
            ],
            name="relay_and_attend",
            compiler_params=pltpu.CompilerParams(
                collective_id=0, has_side_effects=True, vmem_limit_bytes=16 * 2**20
            ),
        )(*arguments)
        return pl.pallas_call(
            last_kernel,
            out_shape=jax.ShapeDtypeStruct(queries.shape, jnp.bfloat16),
            in_specs=[vmem] * 6,
            out_specs=anywhere,
            scratch_shapes=[
                pltpu.VMEM((GROUPS - FIRST, TOK, RATIO * HEAD), jnp.bfloat16),
                pltpu.SemaphoreType.DMA((GROUPS,)),
            ],
            name="attend_and_write",
            compiler_params=pltpu.CompilerParams(vmem_limit_bytes=16 * 2**20),
        )(*handed)

    row = P(("inner", "outer"), None)
    return jax.shard_map(local, mesh=mesh, in_specs=(row, row, row, P(("inner", "outer"))), out_specs=row, check_vma=False)
```

```python
import functools

import jax
import jax.numpy as jnp
from jax import lax
from jax.experimental import pallas as pl
from jax.experimental.pallas import tpu as pltpu
from jax.sharding import PartitionSpec as P

MESH = pl.DeviceIdType.MESH
HEAD = 128
GROUPS = 8
RATIO = 8
TOK = 128
NEAR = 2
OWN = 4
AHEAD = 5
LAG = 4
DIVERT = 8
KEPT = GROUPS - DIVERT
FIRST = GROUPS - 1
MASKED = -1e30
LINK, RELAY, PAIR_NEAR, PAIR_FAR = range(4)
LOG2E = 1.4426950408889634


def group_columns(g):
    return pl.ds(pl.multiple_of(g * RATIO * HEAD, HEAD), RATIO * HEAD)


NEAR_BATCH, FAR_BATCH = 8, 2


def scores(q_at, k, bias, h, batch):
    q, g = q_at
    q = [q[:, pl.ds(pl.multiple_of((g * RATIO + h + i) * HEAD, HEAD), HEAD)] for i in range(batch)]
    s = lax.dot_general(
        jnp.concatenate(q, axis=0), k, (((1,), (1,)), ((), ())), preferred_element_type=jnp.float32
    )
    t = (s * (HEAD**-0.5 * LOG2E)).reshape(batch, TOK, -1) + bias[None]
    return t.reshape(batch * TOK, -1)


def keys_values(kv_at, first, last):
    k = kv_at[first:last, :TOK, :].reshape((last - first) * TOK, HEAD)
    v = kv_at[first:last, TOK:, :].reshape((last - first) * TOK, HEAD)
    return k, v


def attend_near(q_at, kv_at, bias, acc_at, top_at):
    k, v = keys_values(kv_at, NEAR, OWN + 1)
    for h in range(0, RATIO, NEAR_BATCH):
        t = scores(q_at, k, bias[:, NEAR * TOK :], h, NEAR_BATCH)
        top = jnp.max(t, axis=-1, keepdims=True)
        p = jnp.exp2(t - top)
        total = jnp.broadcast_to(jnp.sum(p, axis=-1, keepdims=True), (NEAR_BATCH * TOK, HEAD))
        acc = jnp.concatenate([jnp.dot(p.astype(jnp.bfloat16), v, preferred_element_type=jnp.float32), total], axis=1)
        acc_at[h : h + NEAR_BATCH] = acc.reshape(NEAR_BATCH, TOK, 2 * HEAD)
        top_at[h : h + NEAR_BATCH] = jnp.broadcast_to(top, (NEAR_BATCH * TOK, HEAD)).reshape(NEAR_BATCH, TOK, HEAD)


def attend_far(q_at, kv_at, bias, acc_at, top_at, out_at):
    k, v = keys_values(kv_at, 0, NEAR)
    v = jnp.concatenate([v, jnp.ones_like(v)], axis=1)
    for h in range(0, RATIO, FAR_BATCH):
        t = scores(q_at, k, bias[:, : NEAR * TOK], h, FAR_BATCH)
        old = top_at[h : h + FAR_BATCH].reshape(FAR_BATCH * TOK, HEAD)
        top = jnp.maximum(old, jnp.max(t, axis=-1, keepdims=True))
        p = jnp.exp2(t - jnp.concatenate([top, top], axis=1)).astype(jnp.bfloat16)
        fade = jnp.exp2(old - top)
        acc = acc_at[h : h + FAR_BATCH].reshape(FAR_BATCH * TOK, 2 * HEAD) * jnp.concatenate([fade, fade], axis=1)
        acc = acc + jnp.dot(p, v, preferred_element_type=jnp.float32)
        out = (acc[:, :HEAD] / acc[:, HEAD:]).astype(jnp.bfloat16)
        for i in range(FAR_BATCH):
            out_at[:, (h + i) * HEAD : (h + i + 1) * HEAD] = out[i * TOK : (i + 1) * TOK]


def first_kernel(n, outer, q_hbm, k_hbm, v_hbm, doc_hbm, part, kv, qv, bias, acc, top, kv_in, doc, column, tag, mid, in_sem, q_sem, d_sem, send, recv, tsend, trecv, dsend, drecv):
    b = lax.axis_index("inner") * outer + lax.axis_index("outer")
    core = lax.rem(b, 2)
    sibling = b + 1 - 2 * core
    has_next = b < n - 2
    has_prev = b >= 2
    has_two = b >= 4
    z = lax.rem(b // 2, 8)
    more_rows = b < n - 16
    ahead = AHEAD + (7 - z) // 7 - z // 7
    is_source = (z == 6) & more_rows
    is_middle = (z == 3) & (b >= 16)
    is_target = (z == 0) & (b >= 16)
    after = jnp.minimum(b + 2, n - 2 + core)
    before = jnp.maximum(b - 2, core)

    def at(device):
        return (device // outer, lax.rem(device, outer))

    load_q = pltpu.make_async_copy(q_hbm, qv, q_sem)
    load_k = pltpu.make_async_copy(k_hbm, kv_in.at[0], in_sem.at[0])
    load_v = pltpu.make_async_copy(v_hbm, kv_in.at[1], in_sem.at[1])

    near_src = OWN - 2 * core
    far_src = 2 - 2 * core
    routes = {
        LINK: (OWN, 2, after),
        RELAY: (2, 0, after),
        PAIR_NEAR: (near_src, 3, sibling),
        PAIR_FAR: (far_src, 1, sibling),
    }

    def move(kind, g):
        src, dst, device = routes[kind]
        return pltpu.make_async_remote_copy(
            src_ref=kv.at[g, src],
            dst_ref=kv.at[g, dst],
            send_sem=send.at[kind, g],
            recv_sem=recv.at[kind, g],
            device_id=at(device),
            device_id_type=MESH,
        )

    def move_tag(kind):
        src, dst, device = routes[kind]
        return pltpu.make_async_remote_copy(
            src_ref=tag.at[src],
            dst_ref=tag.at[dst],
            send_sem=tsend.at[kind],
            recv_sem=trecv.at[kind],
            device_id=at(device),
            device_id_type=MESH,
        )

    def to_middle(m):
        return pltpu.make_async_remote_copy(
            src_ref=kv.at[KEPT + m, OWN],
            dst_ref=mid.at[m],
            send_sem=dsend.at[0, m],
            recv_sem=drecv.at[m],
            device_id=at(jnp.minimum(b + 10, n - 1)),
            device_id_type=MESH,
        )

    def from_middle(m):
        return pltpu.make_async_remote_copy(
            src_ref=mid.at[m],
            dst_ref=kv.at[KEPT + m, 0],
            send_sem=dsend.at[1, m],
            recv_sem=recv.at[RELAY, KEPT + m],
            device_id=at(jnp.maximum(b - 6, 0)),
            device_id_type=MESH,
        )

    def relays(g):
        return has_prev & has_next & jnp.logical_not((z == 7) & (g >= KEPT))

    barrier = pltpu.get_barrier_semaphore()

    @pl.when(has_prev)
    def _():
        pl.semaphore_signal(barrier, inc=1, device_id=at(before), device_id_type=MESH)

    @pl.when(is_middle)
    def _():
        pl.semaphore_signal(barrier, inc=1, device_id=at(jnp.maximum(b - 10, 0)), device_id_type=MESH)

    @pl.when(is_target)
    def _():
        pl.semaphore_signal(barrier, inc=1, device_id=at(jnp.minimum(b + 6, n - 1)), device_id_type=MESH)

    pl.semaphore_signal(barrier, inc=1, device_id=at(sibling), device_id_type=MESH)

    doc_copy = pltpu.make_async_copy(doc_hbm, doc, d_sem)
    load_k.start()
    load_v.start()
    doc_copy.start()
    load_q.start()

    @pl.when(jnp.logical_not(has_two))
    def _():
        kv[:, 0] = jnp.zeros((GROUPS, 2 * TOK, HEAD), jnp.bfloat16)
        tag[0] = jnp.full((16, TOK), -1, jnp.bfloat16)

    @pl.when(jnp.logical_not(has_prev))
    def _():
        kv[:, 2] = jnp.zeros((GROUPS, 2 * TOK, HEAD), jnp.bfloat16)
        tag[2] = jnp.full((16, TOK), -1, jnp.bfloat16)

    def when(condition, action):
        pl.when(condition)(action)

    pl.semaphore_wait(barrier, 1 + has_next.astype(jnp.int32) + (is_source | is_middle).astype(jnp.int32))
    load_k.wait()
    load_v.wait()
    for g in range(GROUPS):
        for i in range(2):
            kv[g, OWN, i * TOK : (i + 1) * TOK] = kv_in[i, :, g * HEAD : (g + 1) * HEAD]
        if g < AHEAD + 2:
            when(has_next & (g < ahead), lambda: move(LINK, g).start())
        when(is_source, lambda: to_middle(g).start())
        if g == 0:
            doc_copy.wait()
            docs = jnp.broadcast_to(doc[...].reshape(1, TOK).astype(jnp.float32), (TOK, TOK))
            tag[OWN] = docs[:16].astype(jnp.bfloat16)
            when(has_next, lambda: move_tag(LINK).start())
    column[...] = docs.T
    row = lax.broadcasted_iota(jnp.int32, (TOK, TOK), 0)
    col = lax.broadcasted_iota(jnp.int32, (TOK, TOK), 1)
    bias[:, OWN * TOK :] = jnp.where((column[...] == docs) & (col <= row), 0.0, MASKED)
    def mask(s):
        other = jnp.broadcast_to(tag[s][:1].astype(jnp.float32), (TOK, TOK))
        bias[:, s * TOK : (s + 1) * TOK] = jnp.where(column[...] == other, 0.0, MASKED)

    def step(it, _):
        @pl.when(it == 0)
        def _():
            when(has_prev, lambda: move_tag(LINK).wait_recv())
            when(has_prev & has_next, lambda: move_tag(RELAY).start())
            move_tag(PAIR_NEAR).start()
            when(core == 0, lambda: move_tag(PAIR_FAR).start())

        @pl.when(it < GROUPS)
        def _():
            when(has_prev, lambda: move(LINK, it).wait_recv())
            when(relays(it), lambda: move(RELAY, it).start())
            move(PAIR_NEAR, it).start()
            when(core == 0, lambda: move(PAIR_FAR, it).start())

        when(has_next & (it + ahead < GROUPS), lambda: move(LINK, it + ahead).start())

        def pass_on(m):
            to_middle(m).wait_recv()
            from_middle(m).start()

        @pl.when(is_middle & (it >= 1) & (it < 7))
        def _():
            m = it - 1 + (it // 5)
            pass_on(m)
            when((it == 4) | (it == 6), lambda: pass_on(m + 1))

        @pl.when(it == 1)
        def _():
            load_q.wait()
            move_tag(PAIR_NEAR).wait_recv()
            mask(2)
            mask(3)

        @pl.when((it >= 1) & (it < GROUPS + 1))
        def _():
            g = it - 1
            move(PAIR_NEAR, g).wait_recv()
            attend_near((qv, g), kv.at[g], bias, acc.at[g], top.at[g])

        @pl.when(it == LAG)
        def _():
            when(has_two, lambda: move_tag(RELAY).wait_recv())
            when(core == 1, lambda: move_tag(PAIR_FAR).start())

        @pl.when((it >= LAG) & (it < GROUPS + LAG))
        def _():
            when(has_two, lambda: move(RELAY, it - LAG).wait_recv())
            when(core == 1, lambda: move(PAIR_FAR, it - LAG).start())

        @pl.when(it == LAG + 1)
        def _():
            move_tag(PAIR_FAR).wait_recv()
            mask(0)
            mask(1)

        @pl.when((it > LAG) & (it < FIRST + LAG + 1))
        def _():
            g = it - LAG - 1
            move(PAIR_FAR, g).wait_recv()
            attend_far((qv, g), kv.at[g], bias, acc.at[g], top.at[g], part.at[g])

        return 0

    lax.fori_loop(0, FIRST + LAG + 1, step, 0)

    for kind in routes:
        if kind == LINK:
            when(has_next, lambda: move_tag(LINK).wait_send())
        elif kind == RELAY:
            when(has_prev & has_next, lambda: move_tag(RELAY).wait_send())
        else:
            move_tag(kind).wait_send()

    def finish(g, _):
        when(has_next, lambda: move(LINK, g).wait_send())
        when(relays(g), lambda: move(RELAY, g).wait_send())
        move(PAIR_NEAR, g).wait_send()
        move(PAIR_FAR, g).wait_send()
        return 0

    lax.fori_loop(0, GROUPS, finish, 0)
    for m in range(DIVERT):
        when(is_source, lambda: to_middle(m).wait_send())
        when(is_middle, lambda: from_middle(m).wait_send())
    for g in range(FIRST, GROUPS):
        move(PAIR_FAR, g).wait_recv()


def last_kernel(part, kv, qv, bias, acc, top, o_hbm, out, sem):
    def store(g):
        source = part.at[g] if g < FIRST else out.at[g - FIRST]
        return pltpu.make_async_copy(source, o_hbm.at[:, group_columns(g)], sem.at[g])

    for g in range(FIRST):
        store(g).start()
    for g in range(FIRST, GROUPS):
        attend_far((qv, g), kv.at[g], bias, acc.at[g], top.at[g], out.at[g - FIRST])
        store(g).start()
    for g in range(GROUPS):
        store(g).wait()


def solution(mesh):
    n, outer = mesh.size, mesh.shape["outer"]

    def local(queries, keys, values, documents):
        anywhere = pl.BlockSpec(memory_space=pl.ANY)
        vmem = pl.BlockSpec(memory_space=pltpu.VMEM)
        arguments = [pltpu.with_memory_space_constraint(x, pltpu.HBM) for x in (queries, keys, values, documents)]
        handed = pl.pallas_call(
            functools.partial(first_kernel, n, outer),
            out_shape=(
                pltpu.VMEM((FIRST, TOK, RATIO * HEAD), jnp.bfloat16),
                pltpu.VMEM((GROUPS, 5, 2 * TOK, HEAD), jnp.bfloat16),
                pltpu.VMEM(queries.shape, jnp.bfloat16),
                pltpu.VMEM((TOK, 5 * TOK), jnp.float32),
                pltpu.VMEM((GROUPS, RATIO, TOK, 2 * HEAD), jnp.float32),
                pltpu.VMEM((GROUPS, RATIO, TOK, HEAD), jnp.float32),
            ),
            in_specs=[anywhere] * 4,
            out_specs=(vmem,) * 6,
            scratch_shapes=[
                pltpu.VMEM((2, TOK, GROUPS * HEAD), jnp.bfloat16),
                pltpu.VMEM((TOK,), jnp.int32),
                pltpu.VMEM((TOK, TOK), jnp.float32),
                pltpu.VMEM((5, 16, TOK), jnp.bfloat16),
                pltpu.VMEM((DIVERT, 2 * TOK, HEAD), jnp.bfloat16),
                pltpu.SemaphoreType.DMA((2,)),
                pltpu.SemaphoreType.DMA,
                pltpu.SemaphoreType.DMA,
                pltpu.SemaphoreType.DMA((4, GROUPS)),
                pltpu.SemaphoreType.DMA((4, GROUPS)),
                pltpu.SemaphoreType.DMA((4,)),
                pltpu.SemaphoreType.DMA((4,)),
                pltpu.SemaphoreType.DMA((2, DIVERT)),
                pltpu.SemaphoreType.DMA((DIVERT,)),
            ],
            name="relay_and_attend",
            compiler_params=pltpu.CompilerParams(
                collective_id=0, has_side_effects=True, vmem_limit_bytes=16 * 2**20
            ),
        )(*arguments)
        return pl.pallas_call(
            last_kernel,
            out_shape=jax.ShapeDtypeStruct(queries.shape, jnp.bfloat16),
            in_specs=[vmem] * 6,
            out_specs=anywhere,
            scratch_shapes=[
                pltpu.VMEM((GROUPS - FIRST, TOK, RATIO * HEAD), jnp.bfloat16),
                pltpu.SemaphoreType.DMA((GROUPS,)),
            ],
            name="attend_and_write",
            compiler_params=pltpu.CompilerParams(vmem_limit_bytes=16 * 2**20),
        )(*handed)

    row = P(("inner", "outer"), None)
    return jax.shard_map(local, mesh=mesh, in_specs=(row, row, row, P(("inner", "outer"))), out_specs=row, check_vma=False)
```
